32 devices in a mesh: pool: 2 (over x), hold: 8 (over z, y), head: 2 (over core).
Axes of the slice: x: 2, y: 2, z: 4, core: 2. Of those that a mesh axis runs over, the one named last changes fastest.
Arguments:
- query_nope: bfloat16 [2048, 32, 128], P(('pool', 'hold'), 'head'), parts along dimension 0, may hold values from -6 to 6
- query_rope: bfloat16 [2048, 2048], P(('pool', 'hold'), 'head'), parts along dimension 0, may hold values from -8 to 8
- key_up: bfloat16 [32, 128, 512], P('head'), may hold values from -0.5 to 0.5
- value_up: bfloat16 [32, 512, 128], P('head'), may hold values from -3 to 3
- span_latent: bfloat16 [2048, 512], P(('pool', 'hold')), parts along dimension 0, may hold values from -6 to 6
- span_rope: bfloat16 [64, 2048], P(None, ('pool', 'hold')), parts along dimension 1, may hold values from -8 to 8
- pool_latent: bfloat16 [96, 128, 512], P(('pool', 'hold')), parts along dimension 0, may hold values from -6 to 6
- pool_rope: bfloat16 [96, 64, 128], P(('pool', 'hold')), parts along dimension 0, may hold values from -6 to 6
- hit_holders: int32 [16, 24], P(('pool', 'hold')), parts along dimension 0, may hold values from 0 to 7, as said below
- hit_blocks: int32 [16, 24], P(('pool', 'hold')), parts along dimension 0, may hold values from 0 to 5, as said below
- prefix_len: int32 [16], P(('pool', 'hold')), parts along dimension 0, may hold values from 2305 to 3072, as said below
- span_len: int32 [16], P(('pool', 'hold')), parts along dimension 0, may hold values from 64 to 128, as said below
Outputs:
- attended: bfloat16 [2048, 4096], P(('pool', 'hold'), 'head'), parts along dimension 0
The draws below stay inside these ranges and needn't reach their ends.
There are 2 independent parts, one for each index of `pool`. The reference program is written for one: setup_inputs(seed, part) draws one part's arguments, and reference() takes and returns one part's arrays. A program takes and returns all parts, laid end to end along the dimension named above; an argument that names none is the same for every part. Nothing has to cross between parts.
Inputs may be any that keep to these rules, and one draw needn't show every extreme that they name: `hit_holders`: among one request's 24 entries at most 3 name the same device; in every draw some request takes exactly 3 blocks from one device. `hit_blocks`: entries of one request on one device name distinct slots; different requests may share blocks. `prefix_len`: some request has the full 24 * 128 tokens in every draw. `span_len`: some request has all 128 tokens in every draw.
All inputs are finite; a program needn't handle non-finite values.
Results may differ from the reference program's by a relative error of at most 0.0095.
Values may be sent and summed in bfloat16 or wider, within the bound.
A program may use at most 64 MiB of HBM per device.

```python
import jax
import jax.numpy as jnp
from jax import lax

HEADS = 32
NOPE = 128
ROPE = 64
LAT = 512
VDIM = 128
BLOCK = 128
MAXBLK = 24
BLK_DEV = 6
TOK_DEV = 128
CAP = 3
REQS = 8
TOKENS = 1024
POOL = 48


def hit_tables(key):
    request_keys = jax.random.split(key, REQS)

    def shuffled(request_key):
        return jax.random.permutation(request_key, REQS * CAP)[:MAXBLK]
    slot_ids = jax.vmap(shuffled)(request_keys)
    holders = slot_ids // CAP
    ranks = slot_ids % CAP
    first = jax.random.permutation(jax.random.fold_in(key, 5), REQS)
    entry = jnp.arange(MAXBLK)
    special = jax.random.randint(jax.random.fold_in(key, 7), (), 0, REQS)
    chosen_row = (jnp.arange(REQS) == special)[:, None]
    holders = jnp.where(chosen_row, first[entry // CAP][None, :], holders)
    ranks = jnp.where(chosen_row, (entry % CAP)[None, :], ranks)
    offsets = jax.random.randint(jax.random.fold_in(key, 6), (REQS, REQS), 0, BLK_DEV)
    shifts = jnp.take_along_axis(offsets, holders, axis=1)
    blocks = (ranks + shifts) % BLK_DEV
    return (holders.astype(jnp.int32), blocks.astype(jnp.int32))


def draw_hit_holders(key, part):
    holders, blocks = hit_tables(key)
    return holders


def draw_hit_blocks(key, part):
    holders, blocks = hit_tables(key)
    return blocks


def draw_prefix_len(key, part):
    key = jax.random.fold_in(key, 3)
    longest = MAXBLK * BLOCK
    values = jax.random.randint(key, (REQS,), longest * 3 // 4 + 1, longest + 1)
    special = jax.random.randint(jax.random.fold_in(key, 8), (), 0, REQS)
    return jnp.where(jnp.arange(REQS) == special, longest, values).astype(jnp.int32)


def draw_span_len(key, part):
    key = jax.random.fold_in(key, 4)
    values = jax.random.randint(key, (REQS,), TOK_DEV // 2, TOK_DEV + 1)
    special = jax.random.randint(jax.random.fold_in(key, 9), (), 0, REQS)
    return jnp.where(jnp.arange(REQS) == special, TOK_DEV, values).astype(jnp.int32)


def draw_query_rope(key, part):
    key = jax.random.fold_in(key, 11)
    values = jnp.clip(jax.random.normal(key, (TOKENS, HEADS, ROPE), jnp.float32), -8.0, 8.0)
    return values.reshape(TOKENS, HEADS * ROPE).astype(jnp.bfloat16)


def draw_span_rope(key, part):
    key = jax.random.fold_in(key, 13)
    values = jnp.clip(jax.random.normal(key, (ROPE, TOKENS), jnp.float32), -8.0, 8.0)
    return values.astype(jnp.bfloat16)


def shard_levels(rng, extent, cuts, low, top_value):
    factor_of, own = 1.0, jax.random.fold_in(rng, 6)
    for axis_at, shards_of in cuts:
        heights = jnp.exp(jax.random.uniform(jax.random.fold_in(own, axis_at), (shards_of,), jnp.float32, low / len(cuts), top_value / len(cuts)))
        factor_of = factor_of * jnp.repeat(heights, extent[axis_at] // shards_of).reshape([-1 if axis == axis_at else 1 for axis in range(len(extent))])
    return factor_of


def scatter_about(own_key, shape, deviation, most, shards=(), held_as=jnp.bfloat16):
    values = deviation * jax.random.normal(own_key, shape, jnp.float32)
    if shards:
        values = values * shard_levels(own_key, shape, shards, -0.22, 0.18)
    return jnp.clip(values, -most, most).astype(held_as)


def setup_inputs(seed: int = 0, part: int = 0) -> dict:
    key_list = jax.random.split(jax.random.key(seed), 13)
    own_keys = jax.random.split(jax.random.fold_in(key_list[12], part), 13)
    query_nope = scatter_about(own_keys[0], (TOKENS, HEADS, NOPE), 1.0, 6.0, ((0, 8), (1, 2)))
    query_rope = draw_query_rope(jax.random.fold_in(jax.random.fold_in(key_list[12], part), 71), part)
    key_up = scatter_about(key_list[2], (HEADS, NOPE, LAT), NOPE ** -0.5, 0.5, ((0, 2),))
    value_up = scatter_about(key_list[3], (HEADS, LAT, VDIM), 0.5, 3.0, ((0, 2),))
    span_latent = scatter_about(own_keys[4], (TOKENS, LAT), 1.0, 6.0, ((0, 8),))
    span_rope = draw_span_rope(jax.random.fold_in(jax.random.fold_in(key_list[12], part), 71), part)
    pool_latent = scatter_about(own_keys[6], (POOL, BLOCK, LAT), 1.0, 6.0, ((0, 8),))
    pool_rope = scatter_about(own_keys[7], (POOL, ROPE, BLOCK), 1.0, 6.0, ((0, 8),))
    hit_holders = draw_hit_holders(jax.random.fold_in(jax.random.fold_in(key_list[12], part), 71), part)
    hit_blocks = draw_hit_blocks(jax.random.fold_in(jax.random.fold_in(key_list[12], part), 71), part)
    prefix_len = draw_prefix_len(jax.random.fold_in(jax.random.fold_in(key_list[12], part), 71), part)
    span_len = draw_span_len(jax.random.fold_in(jax.random.fold_in(key_list[12], part), 71), part)
    return {"query_nope": query_nope, "query_rope": query_rope, "key_up": key_up, "value_up": value_up, "span_latent": span_latent, "span_rope": span_rope, "pool_latent": pool_latent, "pool_rope": pool_rope, "hit_holders": hit_holders, "hit_blocks": hit_blocks, "prefix_len": prefix_len, "span_len": span_len}


def attend_request(lat_q, rot_q, keys_lat, keys_rope, visible, value_up, softmax_scale):
    scores = jnp.einsum("htl,kl->htk", lat_q.astype(jnp.float32), keys_lat.astype(jnp.float32))
    scores = scores + jnp.einsum("htr,rk->htk", rot_q.astype(jnp.float32), keys_rope.astype(jnp.float32))
    scores = jnp.where(visible[None], scores * softmax_scale, -jnp.inf)
    row_peak = jnp.max(scores, axis=2, keepdims=True)
    weights = jnp.exp(scores - row_peak)
    probabilities = (weights / jnp.sum(weights, axis=2, keepdims=True)).astype(jnp.bfloat16)
    mixed_lat = jnp.einsum("htk,kl->htl", probabilities.astype(jnp.float32), keys_lat.astype(jnp.float32)).astype(jnp.bfloat16)
    return jnp.einsum("htl,hlv->htv", mixed_lat.astype(jnp.float32), value_up.astype(jnp.float32))


def reference(query_nope, query_rope, key_up, value_up, span_latent, span_rope, pool_latent, pool_rope, hit_holders, hit_blocks, prefix_len, span_len):
    softmax_scale = float(NOPE + ROPE) ** -0.5
    query_latent = jnp.einsum("thn,hnl->thl", query_nope.astype(jnp.float32), key_up.astype(jnp.float32)).astype(jnp.bfloat16)
    query_latent = query_latent.reshape(REQS, TOK_DEV, HEADS, LAT).transpose(0, 2, 1, 3)
    query_rot = query_rope.reshape(REQS, TOK_DEV, HEADS, ROPE).transpose(0, 2, 1, 3)
    new_latent = span_latent.reshape(REQS, TOK_DEV, LAT)
    new_rope = span_rope.reshape(ROPE, REQS, TOK_DEV).transpose(1, 0, 2)
    places = jnp.arange(MAXBLK * BLOCK, dtype=jnp.int32)
    row_index = jnp.arange(TOK_DEV, dtype=jnp.int32)
    causal = row_index[None, :] <= row_index[:, None]

    def one_request(inputs):
        lat_q, rot_q, lat_new, rope_new, holders, blocks, prefix_tokens, span_count = inputs
        pool_index = (holders * BLK_DEV + blocks).astype(jnp.int32)
        keys_lat = jnp.concatenate([pool_latent[pool_index].reshape(MAXBLK * BLOCK, LAT), lat_new], axis=0)
        old_rope = pool_rope[pool_index].transpose(1, 0, 2).reshape(ROPE, MAXBLK * BLOCK)
        keys_rope = jnp.concatenate([old_rope, rope_new], axis=1)
        prefix_seen = jnp.broadcast_to((places < prefix_tokens)[None, :], (TOK_DEV, MAXBLK * BLOCK))
        visible = jnp.concatenate([prefix_seen, causal], axis=1)
        result = attend_request(lat_q, rot_q, keys_lat, keys_rope, visible, value_up, softmax_scale)
        result = jnp.where((row_index < span_count)[None, :, None], result, 0.0)
        return result.transpose(1, 0, 2).reshape(TOK_DEV, HEADS * VDIM).astype(jnp.bfloat16)

    outputs = lax.map(one_request, (query_latent, query_rot, new_latent, new_rope, hit_holders, hit_blocks, prefix_len, span_len))
    return outputs.reshape(TOKENS, HEADS * VDIM)
```

```python
import functools
import math

import jax
import jax.numpy as jnp
from jax import lax
from jax.experimental import pallas as pl
from jax.experimental.pallas import tpu as pltpu
from jax.sharding import PartitionSpec as P

MESH = pl.DeviceIdType.MESH
MASKED = -1e30


def send_order(holders):
    near = list(range(1, holders // 2))
    far = list(range(holders // 2, holders))
    order = []
    while near or far:
        if near:
            order.append(near.pop(0))
        if far:
            order.append(far.pop(0))
    return order


def kernel(
    sizes,
    table_ref,
    bias_ref,
    count_ref,
    pool_lat,
    pool_rope,
    span_lat,
    span_rope,
    nope_hbm,
    rope_q,
    key_up_hbm,
    value_up_hbm,
    out_ref,
    table_in,
    table_smem,
    send_lat,
    send_rope,
    kv,
    kr,
    nope,
    nope32,
    key_up,
    value_up,
    q_lat,
    q_aug,
    acc,
    peak,
    total,
    local_sem,
    table_send,
    table_recv,
    lat_send,
    lat_recv,
    rope_send,
    rope_recv,
    fwd_lat_send,
    fwd_lat_recv,
    fwd_rope_send,
    fwd_rope_recv,
):
    holders, slots, heads, toks, block, lat, rope, scale = sizes
    width = slots * block
    half = lat // 2
    rope_half = rope // 2
    pool, me, core = lax.axis_index("pool"), lax.axis_index("hold"), lax.axis_index("head")
    other = 1 - core
    sibling = (pool, me, other)
    order = send_order(holders)
    base = {0: toks}
    for at, k in enumerate(order):
        base[k] = toks + (at + 1) * width

    def peer(k):
        return (pool, me ^ k, core)

    loads = [
        pltpu.make_async_copy(nope_hbm, nope, local_sem.at[0]),
        pltpu.make_async_copy(key_up_hbm, key_up, local_sem.at[1]),
        pltpu.make_async_copy(value_up_hbm, value_up, local_sem.at[2]),
    ]
    for load in loads:
        load.start()

    barrier = pltpu.get_barrier_semaphore()
    for k in order:
        pl.semaphore_signal(barrier, inc=1, device_id=peer(k), device_id_type=MESH)
    pl.semaphore_signal(barrier, inc=1, device_id=sibling, device_id_type=MESH)
    pl.semaphore_wait(barrier, holders)

    tables = []
    for k in order:
        copy = pltpu.make_async_remote_copy(
            src_ref=table_ref.at[me ^ k],
            dst_ref=table_in.at[k],
            send_sem=table_send.at[k],
            recv_sem=table_recv.at[k],
            device_id=peer(k),
            device_id_type=MESH,
        )
        copy.start()
        tables.append(copy)
    table_in[0] = table_ref[me]
    for copy in tables:
        copy.wait_recv()
    to_smem = pltpu.make_async_copy(table_in, table_smem, local_sem.at[3])
    to_smem.start()
    to_smem.wait()

    copies = {}
    for k in order:
        for s in range(slots):
            b = table_smem[k, 0, s]
            rows = pl.ds(s * block, block)
            send_lat[k, rows, :] = pool_lat[b, :, pl.ds(pl.multiple_of(core * half, half), half)]
            send_rope[k, :, rows] = pool_rope[
                b, pl.ds(pl.multiple_of(core * rope_half, rope_half), rope_half), :
            ]
        lat_copy = pltpu.make_async_remote_copy(
            src_ref=send_lat.at[k],
            dst_ref=kv.at[core, pl.ds(base[k], width), :],
            send_sem=lat_send.at[k],
            recv_sem=lat_recv.at[k],
            device_id=peer(k),
            device_id_type=MESH,
        )
        rope_copy = pltpu.make_async_remote_copy(
            src_ref=send_rope.at[k],
            dst_ref=kr.at[
                pl.ds(pl.multiple_of(core * rope_half, rope_half), rope_half), pl.ds(base[k], width)
            ],
            send_sem=rope_send.at[k],
            recv_sem=rope_recv.at[k],
            device_id=peer(k),
            device_id_type=MESH,
        )
        lat_copy.start()
        rope_copy.start()
        copies[k] = (lat_copy, rope_copy)

    for c in range(2):
        kv[c, pl.ds(0, toks), :] = span_lat[:, c * half : (c + 1) * half]
    kr[pl.ds(0, rope), pl.ds(0, toks)] = span_rope[...]
    kr[pl.ds(rope, 128 - rope), :] = jnp.zeros((128 - rope, kr.shape[1]), jnp.bfloat16)
    for s in range(slots):
        b = table_smem[0, 0, s]
        for c in range(2):
            kv[c, pl.ds(toks + s * block, block), :] = pool_lat[b, :, c * half : (c + 1) * half]
        kr[pl.ds(0, rope), pl.ds(toks + s * block, block)] = pool_rope[b]
    for k in [0] + order:
        kr[pl.ds(rope, 16), pl.ds(base[k], width)] = bias_ref[me ^ k]

    loads[0].wait()
    loads[1].wait()
    nope32[...] = nope[...].astype(jnp.float32)
    one_col = (lax.broadcasted_iota(jnp.int32, (toks, 128 - rope), 1) == 0).astype(jnp.bfloat16)
    for h in range(heads):
        q_h = nope32[pl.ds(h, toks, stride=heads), :].astype(jnp.bfloat16)
        up = jnp.dot(q_h, key_up[h], preferred_element_type=jnp.float32)
        q_lat[pl.ds(h * toks, toks), :] = (up * scale).astype(jnp.bfloat16)
        rot = rope_q[:, h * rope : (h + 1) * rope].astype(jnp.float32) * scale
        q_aug[pl.ds(h * toks, toks), :] = jnp.concatenate([rot.astype(jnp.bfloat16), one_col], axis=1)

    tile = 2 * toks
    tiles = heads // 2
    nt = (((1,), (1,)), ((), ()))

    def attend(start, size, first):
        keys = pl.ds(start, size)

        def one(t, carry):
            rows = pl.ds(pl.multiple_of(t * tile, tile), tile)
            s = lax.dot_general(
                q_lat[rows, 0:half], kv[0, keys, :], nt, preferred_element_type=jnp.float32
            )
            s += lax.dot_general(
                q_lat[rows, half:lat], kv[1, keys, :], nt, preferred_element_type=jnp.float32
            )
            s += jnp.dot(q_aug[rows, :], kr[:, keys], preferred_element_type=jnp.float32)
            if first:
                row = lax.broadcasted_iota(jnp.int32, (tile, size), 0) % toks
                col = lax.broadcasted_iota(jnp.int32, (tile, size), 1)
                s = jnp.where((col <= row) | (col >= toks), s, MASKED)
            top = jnp.max(s, axis=1, keepdims=True)
            if not first:
                old = peak[rows, :]
                top = jnp.maximum(top, old)
                alpha = jnp.exp2(old - top)
            p = jnp.exp2(s - top)
            summed = jnp.sum(p, axis=1, keepdims=True)
            p = p.astype(jnp.bfloat16)
            peak[rows, :] = top
            total[rows, :] = summed if first else total[rows, :] * alpha + summed
            for c in range(2):
                cols = pl.ds(c * half, half)
                mixed = jnp.dot(p, kv[c, keys, :], preferred_element_type=jnp.float32)
                acc[rows, cols] = mixed if first else acc[rows, cols] * alpha + mixed
            return carry

        lax.fori_loop(0, tiles, one, 0, unroll=2)

    attend(0, toks + width, True)

    forwards = []
    group = max(1, 768 // width)
    for at in range(0, len(order), group):
        members = order[at : at + group]
        current = []
        for k in members:
            copies[k][0].wait_recv()
            copies[k][1].wait_recv()
            lat_rows = kv.at[core, pl.ds(base[k], width), :]
            rope_rows = kr.at[
                pl.ds(pl.multiple_of(core * rope_half, rope_half), rope_half), pl.ds(base[k], width)
            ]
            lat_fwd = pltpu.make_async_remote_copy(
                src_ref=lat_rows,
                dst_ref=lat_rows,
                send_sem=fwd_lat_send.at[k],
                recv_sem=fwd_lat_recv.at[k],
                device_id=sibling,
                device_id_type=MESH,
            )
            rope_fwd = pltpu.make_async_remote_copy(
                src_ref=rope_rows,
                dst_ref=rope_rows,
                send_sem=fwd_rope_send.at[k],
                recv_sem=fwd_rope_recv.at[k],
                device_id=sibling,
                device_id_type=MESH,
            )
            lat_fwd.start()
            rope_fwd.start()
            current += [lat_fwd, rope_fwd]
        for copy in current:
            copy.wait_recv()
        forwards += current
        attend(base[members[0]], len(members) * width, False)

    loads[2].wait()
    live = lax.broadcasted_iota(jnp.int32, (toks, value_up.shape[2]), 0) < count_ref[0]
    for h in range(heads):
        rows = pl.ds(h * toks, toks)
        mixed = (acc[rows, :] / total[rows, :]).astype(jnp.bfloat16)
        up = jnp.dot(mixed, value_up[h], preferred_element_type=jnp.float32)
        vdim = value_up.shape[2]
        out_ref[:, h * vdim : (h + 1) * vdim] = jnp.where(live, up, 0.0).astype(out_ref.dtype)

    for copy in tables + forwards:
        copy.wait_send()
    for k in order:
        copies[k][0].wait_send()
        copies[k][1].wait_send()


def on_device(
    query_nope,
    query_rope,
    key_up,
    value_up,
    span_latent,
    span_rope,
    pool_latent,
    pool_rope,
    hit_holders,
    hit_blocks,
    prefix_len,
    span_len,
):
    holders = lax.axis_size("hold")
    toks, heads, nope_width = query_nope.shape
    lat = key_up.shape[2]
    rope = span_rope.shape[0]
    block = pool_latent.shape[1]
    list_len = hit_holders.shape[1]
    vdim = value_up.shape[2]
    slots = (list_len + holders - 1) // holders
    width = slots * block
    scale = float(nope_width + rope) ** (-0.5) * math.log2(math.e)

    row = hit_holders[0]
    entry = jnp.arange(list_len)
    rank = jnp.sum((row[:, None] == row[None, :]) & (entry[None, :] < entry[:, None]), axis=1)
    match = (row[None, None, :] == jnp.arange(holders)[:, None, None]) & (
        rank[None, None, :] == jnp.arange(slots)[None, :, None]
    )
    ids = jnp.sum(jnp.where(match, hit_blocks[0][None, None, :], 0), axis=2)
    table = jnp.broadcast_to(
        jnp.pad(ids, ((0, 0), (0, 128 - slots)))[:, None, :], (holders, 8, 128)
    ).astype(jnp.int32)
    seen = jnp.sum(jnp.where(match, jnp.maximum(prefix_len[0] - entry * block, 0), 0), axis=2)
    hidden = jnp.arange(block)[None, None, :] >= seen[:, :, None]
    bias = jnp.where(hidden, MASKED, 0.0).reshape(holders, 1, width)
    first_row = jnp.arange(16)[None, :, None] == 0
    bias = jnp.where(first_row, bias, 0.0).astype(jnp.bfloat16)

    keys = toks + holders * width
    rows = heads * toks
    vmem = pl.BlockSpec(memory_space=pltpu.VMEM)
    any_space = pl.BlockSpec(memory_space=pl.ANY)
    sems = pltpu.SemaphoreType.DMA((holders,))
    sizes = (holders, slots, heads, toks, block, lat, rope, scale)
    return pl.pallas_call(
        functools.partial(kernel, sizes),
        out_shape=jax.ShapeDtypeStruct((toks, heads * vdim), jnp.bfloat16),
        in_specs=[
            vmem,
            vmem,
            pl.BlockSpec(memory_space=pltpu.SMEM),
            vmem,
            vmem,
            vmem,
            vmem,
            any_space,
            vmem,
            any_space,
            any_space,
        ],
        out_specs=vmem,
        scratch_shapes=[
            pltpu.VMEM((holders, 8, 128), jnp.int32),
            pltpu.SMEM((holders, 8, 128), jnp.int32),
            pltpu.VMEM((holders, width, lat // 2), jnp.bfloat16),
            pltpu.VMEM((holders, rope // 2, width), jnp.bfloat16),
            pltpu.VMEM((2, keys, lat // 2), jnp.bfloat16),
            pltpu.VMEM((128, keys), jnp.bfloat16),
            pltpu.VMEM((rows, nope_width), jnp.bfloat16),
            pltpu.VMEM((rows, nope_width), jnp.float32),
            pltpu.VMEM(key_up.shape, jnp.bfloat16),
            pltpu.VMEM(value_up.shape, jnp.bfloat16),
            pltpu.VMEM((rows, lat), jnp.bfloat16),
            pltpu.VMEM((rows, 128), jnp.bfloat16),
            pltpu.VMEM((rows, lat), jnp.float32),
            pltpu.VMEM((rows, 1), jnp.float32),
            pltpu.VMEM((rows, 1), jnp.float32),
            pltpu.SemaphoreType.DMA((4,)),
        ]
        + [sems] * 10,
        compiler_params=pltpu.CompilerParams(
            collective_id=0, has_side_effects=True, vmem_limit_bytes=48 * 1024 * 1024
        ),
    )(
        table,
        bias,
        span_len,
        pool_latent,
        pool_rope,
        span_latent,
        span_rope,
        query_nope.reshape(rows, nope_width),
        query_rope,
        key_up,
        value_up,
    )


def solution(mesh):
    return jax.shard_map(
        on_device,
        mesh=mesh,
        in_specs=(
            P(("pool", "hold"), "head", None),
            P(("pool", "hold"), "head"),
            P("head", None, None),
            P("head", None, None),
            P(("pool", "hold"), None),
            P(None, ("pool", "hold")),
            P(("pool", "hold"), None, None),
            P(("pool", "hold"), None, None),
            P(("pool", "hold"), None),
            P(("pool", "hold"), None),
            P(("pool", "hold")),
            P(("pool", "hold")),
        ),
        out_specs=P(("pool", "hold"), "head"),
        check_vma=False,
    )
```

```python
import functools
import math

import jax
import jax.numpy as jnp
from jax import lax
from jax.experimental import pallas as pl
from jax.experimental.pallas import tpu as pltpu
from jax.sharding import PartitionSpec as P

MESH = pl.DeviceIdType.MESH
MASKED = -1e30


def send_order(holders):
    near = list(range(1, holders // 2))
    far = list(range(holders // 2, holders))
    order = []
    while near or far:
        if near:
            order.append(near.pop(0))
        if far:
            order.append(far.pop(0))
    return order


def kernel(
    sizes,
    table_hbm,
    bias_hbm,
    count_ref,
    pool_lat_hbm,
    pool_rope_hbm,
    span_lat_hbm,
    span_rope_hbm,
    nope_hbm,
    rope_q_hbm,
    key_up_hbm,
    value_up_hbm,
    out_ref,
    table_ref,
    bias_ref,
    pool_lat,
    pool_rope,
    span_lat,
    span_rope,
    rope_q,
    table_in,
    table_smem,
    send_lat,
    send_rope,
    kv,
    kt,
    nope,
    nope32,
    key_up,
    value_up,
    q_all,
    acc,
    peak,
    total,
    local_sem,
    table_send,
    table_recv,
    lat_send,
    lat_recv,
    rope_send,
    rope_recv,
    fwd_lat_send,
    fwd_lat_recv,
    fwd_rope_send,
    fwd_rope_recv,
):
    holders, slots, heads, toks, block, lat, rope, scale = sizes
    width = slots * block
    half = lat // 2
    rope_half = rope // 2
    pool, me, core = lax.axis_index("pool"), lax.axis_index("hold"), lax.axis_index("head")
    other = 1 - core
    sibling = (pool, me, other)
    kr = kt.at[pl.ds(lat, 128), :]
    order = send_order(holders)
    base = {0: toks}
    for at, k in enumerate(order):
        base[k] = toks + (at + 1) * width

    def peer(k):
        return (pool, me ^ k, core)

    pairs = [
        (table_hbm, table_ref),
        (pool_lat_hbm, pool_lat),
        (pool_rope_hbm, pool_rope),
        (span_lat_hbm, span_lat),
        (span_rope_hbm, span_rope),
        (bias_hbm, bias_ref),
        (nope_hbm, nope),
        (key_up_hbm, key_up),
        (rope_q_hbm, rope_q),
        (value_up_hbm, value_up),
    ]
    loads = []
    for at, (src, dst) in enumerate(pairs):
        load = pltpu.make_async_copy(src, dst, local_sem.at[at])
        load.start()
        loads.append(load)

    barrier = pltpu.get_barrier_semaphore()
    for k in order:
        pl.semaphore_signal(barrier, inc=1, device_id=peer(k), device_id_type=MESH)
    pl.semaphore_signal(barrier, inc=1, device_id=sibling, device_id_type=MESH)
    pl.semaphore_wait(barrier, holders)

    loads[0].wait()
    tables = []
    for k in order:
        copy = pltpu.make_async_remote_copy(
            src_ref=table_ref.at[me ^ k],
            dst_ref=table_in.at[k],
            send_sem=table_send.at[k],
            recv_sem=table_recv.at[k],
            device_id=peer(k),
            device_id_type=MESH,
        )
        copy.start()
        tables.append(copy)
    table_in[0] = table_ref[me]
    for copy in tables:
        copy.wait_recv()
    to_smem = pltpu.make_async_copy(table_in, table_smem, local_sem.at[len(pairs)])
    to_smem.start()
    to_smem.wait()

    copies = {}
    loads[1].wait()
    loads[2].wait()
    for k in order:
        for s in range(slots):
            b = table_smem[k, 0, s]
            rows = pl.ds(s * block, block)
            send_lat[k, rows, :] = pool_lat[b, :, pl.ds(pl.multiple_of(core * half, half), half)]
            send_rope[k, :, rows] = pool_rope[
                b, pl.ds(pl.multiple_of(core * rope_half, rope_half), rope_half), :
            ]
        lat_copy = pltpu.make_async_remote_copy(
            src_ref=send_lat.at[k],
            dst_ref=kv.at[core, pl.ds(base[k], width), :],
            send_sem=lat_send.at[k],
            recv_sem=lat_recv.at[k],
            device_id=peer(k),
            device_id_type=MESH,
        )
        rope_copy = pltpu.make_async_remote_copy(
            src_ref=send_rope.at[k],
            dst_ref=kr.at[
                pl.ds(pl.multiple_of(core * rope_half, rope_half), rope_half), pl.ds(base[k], width)
            ],
            send_sem=rope_send.at[k],
            recv_sem=rope_recv.at[k],
            device_id=peer(k),
            device_id_type=MESH,
        )
        lat_copy.start()
        rope_copy.start()
        copies[k] = (lat_copy, rope_copy)

    for at in range(3, 9):
        loads[at].wait()
    for c in range(2):
        kv[c, pl.ds(0, toks), :] = span_lat[:, c * half : (c + 1) * half]
    kr[pl.ds(0, rope), pl.ds(0, toks)] = span_rope[...]
    kr[pl.ds(rope, 128 - rope), :] = jnp.zeros((128 - rope, kr.shape[1]), jnp.bfloat16)
    for s in range(slots):
        b = table_smem[0, 0, s]
        for c in range(2):
            kv[c, pl.ds(toks + s * block, block), :] = pool_lat[b, :, c * half : (c + 1) * half]
        kr[pl.ds(0, rope), pl.ds(toks + s * block, block)] = pool_rope[b]
    for k in [0] + order:
        kr[pl.ds(rope, 16), pl.ds(base[k], width)] = bias_ref[me ^ k]

    nope32[...] = nope[...].astype(jnp.float32)
    one_col = (lax.broadcasted_iota(jnp.int32, (toks, 128 - rope), 1) == 0).astype(jnp.bfloat16)
    for h in range(heads):
        q_h = nope32[pl.ds(h, toks, stride=heads), :].astype(jnp.bfloat16)
        up = jnp.dot(q_h, key_up[h], preferred_element_type=jnp.float32)
        q_all[pl.ds(h * toks, toks), 0:lat] = (up * scale).astype(jnp.bfloat16)
        rot = rope_q[:, h * rope : (h + 1) * rope].astype(jnp.float32) * scale
        q_all[pl.ds(h * toks, toks), lat:] = jnp.concatenate(
            [rot.astype(jnp.bfloat16), one_col], axis=1
        )

    tile = 8 * toks
    tiles = heads // 8

    def attend(start, size, first):
        keys = pl.ds(start, size)
        for c in range(2):
            kt[c * half : (c + 1) * half, keys] = kv[c, keys, :].T

        def one(t, carry):
            rows = pl.ds(pl.multiple_of(t * tile, tile), tile)
            s = jnp.dot(q_all[rows, :], kt[:, keys], preferred_element_type=jnp.float32)
            if first:
                row = lax.broadcasted_iota(jnp.int32, (tile, size), 0) % toks
                col = lax.broadcasted_iota(jnp.int32, (tile, size), 1)
                s = jnp.where((col <= row) | (col >= toks), s, MASKED)
            top = jnp.max(s, axis=1, keepdims=True)
            if not first:
                old = peak[rows, :]
                top = jnp.maximum(top, old)
                alpha = jnp.exp2(old - top)
            p = jnp.exp2(s - top)
            summed = jnp.sum(p, axis=1, keepdims=True)
            p = p.astype(jnp.bfloat16)
            peak[rows, :] = top
            total[rows, :] = summed if first else total[rows, :] * alpha + summed
            for c in range(2):
                cols = pl.ds(c * half, half)
                mixed = jnp.dot(p, kv[c, keys, :], preferred_element_type=jnp.float32)
                acc[rows, cols] = mixed if first else acc[rows, cols] * alpha + mixed
            return carry

        lax.fori_loop(0, tiles, one, 0)

    attend(0, toks + width, True)

    forwards = []
    group = max(1, 768 // width)
    for at in range(0, len(order), group):
        members = order[at : at + group]
        current = []
        for k in members:
            copies[k][0].wait_recv()
            copies[k][1].wait_recv()
            lat_rows = kv.at[core, pl.ds(base[k], width), :]
            rope_rows = kr.at[
                pl.ds(pl.multiple_of(core * rope_half, rope_half), rope_half), pl.ds(base[k], width)
            ]
            lat_fwd = pltpu.make_async_remote_copy(
                src_ref=lat_rows,
                dst_ref=lat_rows,
                send_sem=fwd_lat_send.at[k],
                recv_sem=fwd_lat_recv.at[k],
                device_id=sibling,
                device_id_type=MESH,
            )
            rope_fwd = pltpu.make_async_remote_copy(
                src_ref=rope_rows,
                dst_ref=rope_rows,
                send_sem=fwd_rope_send.at[k],
                recv_sem=fwd_rope_recv.at[k],
                device_id=sibling,
                device_id_type=MESH,
            )
            lat_fwd.start()
            rope_fwd.start()
            current += [lat_fwd, rope_fwd]
        for copy in current:
            copy.wait_recv()
        forwards += current
        attend(base[members[0]], len(members) * width, False)

    loads[9].wait()
    live = lax.broadcasted_iota(jnp.int32, (toks, value_up.shape[2]), 0) < count_ref[0]
    for h in range(heads):
        rows = pl.ds(h * toks, toks)
        mixed = (acc[rows, :] / total[rows, :]).astype(jnp.bfloat16)
        up = jnp.dot(mixed, value_up[h], preferred_element_type=jnp.float32)
        vdim = value_up.shape[2]
        out_ref[:, h * vdim : (h + 1) * vdim] = jnp.where(live, up, 0.0).astype(out_ref.dtype)

    for copy in tables + forwards:
        copy.wait_send()
    for k in order:
        copies[k][0].wait_send()
        copies[k][1].wait_send()


def on_device(
    query_nope,
    query_rope,
    key_up,
    value_up,
    span_latent,
    span_rope,
    pool_latent,
    pool_rope,
    hit_holders,
    hit_blocks,
    prefix_len,
    span_len,
):
    holders = lax.axis_size("hold")
    toks, heads, nope_width = query_nope.shape
    lat = key_up.shape[2]
    rope = span_rope.shape[0]
    block = pool_latent.shape[1]
    list_len = hit_holders.shape[1]
    vdim = value_up.shape[2]
    slots = (list_len + holders - 1) // holders
    width = slots * block
    scale = float(nope_width + rope) ** (-0.5) * math.log2(math.e)

    row = hit_holders[0]
    entry = jnp.arange(list_len)
    rank = jnp.sum((row[:, None] == row[None, :]) & (entry[None, :] < entry[:, None]), axis=1)
    match = (row[None, None, :] == jnp.arange(holders)[:, None, None]) & (
        rank[None, None, :] == jnp.arange(slots)[None, :, None]
    )
    ids = jnp.sum(jnp.where(match, hit_blocks[0][None, None, :], 0), axis=2)
    table = jnp.broadcast_to(
        jnp.pad(ids, ((0, 0), (0, 128 - slots)))[:, None, :], (holders, 8, 128)
    ).astype(jnp.int32)
    seen = jnp.sum(jnp.where(match, jnp.maximum(prefix_len[0] - entry * block, 0), 0), axis=2)
    hidden = jnp.arange(block)[None, None, :] >= seen[:, :, None]
    bias = jnp.where(hidden, MASKED, 0.0).reshape(holders, 1, width)
    first_row = jnp.arange(16)[None, :, None] == 0
    bias = jnp.where(first_row, bias, 0.0).astype(jnp.bfloat16)

    keys = toks + holders * width
    rows = heads * toks
    vmem = pl.BlockSpec(memory_space=pltpu.VMEM)
    any_space = pl.BlockSpec(memory_space=pl.ANY)
    sems = pltpu.SemaphoreType.DMA((holders,))
    sizes = (holders, slots, heads, toks, block, lat, rope, scale)
    return pl.pallas_call(
        functools.partial(kernel, sizes),
        out_shape=jax.ShapeDtypeStruct((toks, heads * vdim), jnp.bfloat16),
        in_specs=[any_space] * 2 + [pl.BlockSpec(memory_space=pltpu.SMEM)] + [any_space] * 8,
        out_specs=vmem,
        scratch_shapes=[
            pltpu.VMEM(table.shape, jnp.int32),
            pltpu.VMEM(bias.shape, jnp.bfloat16),
            pltpu.VMEM(pool_latent.shape, jnp.bfloat16),
            pltpu.VMEM(pool_rope.shape, jnp.bfloat16),
            pltpu.VMEM(span_latent.shape, jnp.bfloat16),
            pltpu.VMEM(span_rope.shape, jnp.bfloat16),
            pltpu.VMEM(query_rope.shape, jnp.bfloat16),
            pltpu.VMEM((holders, 8, 128), jnp.int32),
            pltpu.SMEM((holders, 8, 128), jnp.int32),
            pltpu.VMEM((holders, width, lat // 2), jnp.bfloat16),
            pltpu.VMEM((holders, rope // 2, width), jnp.bfloat16),
            pltpu.VMEM((2, keys, lat // 2), jnp.bfloat16),
            pltpu.VMEM((lat + 128, keys), jnp.bfloat16),
            pltpu.VMEM((rows, nope_width), jnp.bfloat16),
            pltpu.VMEM((rows, nope_width), jnp.float32),
            pltpu.VMEM(key_up.shape, jnp.bfloat16),
            pltpu.VMEM(value_up.shape, jnp.bfloat16),
            pltpu.VMEM((rows, lat + 128), jnp.bfloat16),
            pltpu.VMEM((rows, lat), jnp.float32),
            pltpu.VMEM((rows, 1), jnp.float32),
            pltpu.VMEM((rows, 1), jnp.float32),
            pltpu.SemaphoreType.DMA((11,)),
        ]
        + [sems] * 10,
        compiler_params=pltpu.CompilerParams(
            collective_id=0, has_side_effects=True, vmem_limit_bytes=56 * 1024 * 1024
        ),
    )(
        table,
        bias,
        span_len,
        pool_latent,
        pool_rope,
        span_latent,
        span_rope,
        query_nope.reshape(rows, nope_width),
        query_rope,
        key_up,
        value_up,
    )


def solution(mesh):
    return jax.shard_map(
        on_device,
        mesh=mesh,
        in_specs=(
            P(("pool", "hold"), "head", None),
            P(("pool", "hold"), "head"),
            P("head", None, None),
            P("head", None, None),
            P(("pool", "hold"), None),
            P(None, ("pool", "hold")),
            P(("pool", "hold"), None, None),
            P(("pool", "hold"), None, None),
            P(("pool", "hold"), None),
            P(("pool", "hold"), None),
            P(("pool", "hold")),
            P(("pool", "hold")),
        ),
        out_specs=P(("pool", "hold"), "head"),
        check_vma=False,
    )
```

```python
import functools
import math

import jax
import jax.numpy as jnp
from jax import lax
from jax.experimental import pallas as pl
from jax.experimental.pallas import tpu as pltpu
from jax.sharding import PartitionSpec as P

MESH = pl.DeviceIdType.MESH
MASKED = -1e30


def send_order(holders):
    near = list(range(1, holders // 2))
    far = list(range(holders // 2, holders))
    order = []
    while near or far:
        if near:
            order.append(near.pop(0))
        if far:
            order.append(far.pop(0))
    return order


def kernel(
    sizes,
    table_hbm,
    bias_hbm,
    count_ref,
    pool_lat_hbm,
    pool_rope_hbm,
    span_lat_hbm,
    span_rope_hbm,
    nope_hbm,
    rope_q_hbm,
    key_up_hbm,
    value_up_hbm,
    out_ref,
    table_ref,
    bias_ref,
    pool_lat,
    pool_rope,
    span_lat,
    span_rope,
    rope_q,
    table_in,
    table_smem,
    send_lat,
    send_rope,
    kv,
    kt,
    nope,
    nope32,
    key_up,
    value_up,
    q_all,
    acc,
    peak,
    total,
    local_sem,
    table_send,
    table_recv,
    lat_send,
    lat_recv,
    rope_send,
    rope_recv,
    fwd_lat_send,
    fwd_lat_recv,
    fwd_rope_send,
    fwd_rope_recv,
    *line_refs,
):
    holders, slots, heads, toks, block, lat, rope, scale, line = sizes
    width = slots * block
    half = lat // 2
    rope_half = rope // 2
    pool, me, core = lax.axis_index("pool"), lax.axis_index("hold"), lax.axis_index("head")
    other = 1 - core
    sibling = (pool, me, other)
    kr = kt.at[pl.ds(lat, 128), :]
    order = send_order(holders)
    base = {0: toks}
    for at, k in enumerate(order):
        base[k] = toks + (at + 1) * width

    def peer(k):
        return (pool, me ^ k, core)

    pairs = [
        (table_hbm, table_ref),
        (pool_lat_hbm, pool_lat),
        (pool_rope_hbm, pool_rope),
        (span_lat_hbm, span_lat),
        (span_rope_hbm, span_rope),
        (bias_hbm, bias_ref),
        (nope_hbm, nope),
        (key_up_hbm, key_up),
        (rope_q_hbm, rope_q),
        (value_up_hbm, value_up),
    ]
    loads = []
    for at, (src, dst) in enumerate(pairs):
        load = pltpu.make_async_copy(src, dst, local_sem.at[at])
        load.start()
        loads.append(load)

    if line:
        z, y = me // 2, me % 2
        partner = (pool, me ^ 1, core)
        col_lat, col_rope = line_refs[: line - 1], line_refs[line - 1 : 2 * (line - 1)]
        (tables_in, tables_smem, own_send, relay_send, col_recv, y_send, y_recv, fwd_send, fwd_recv) = (
            line_refs[2 * (line - 1) :]
        )
        sources = [sorted(range(line), key=lambda s, at=at: (abs(s - at), s)) for at in range(line)]
        core_cols = pl.ds(pl.multiple_of(core * half, half), half)
        core_rope = pl.ds(pl.multiple_of(core * rope_half, rope_half), rope_half)

        def source_of(n):
            code = sum(sources[at][n] << (4 * at) for at in range(line))
            return (code >> (4 * z)) & 15

        def to_line(at, target, src_lat, src_rope, source, send_sems):
            n = sources[target].index(source) - 1
            device = (pool, target * 2 + y, core)
            return [
                pltpu.make_async_remote_copy(
                    src_ref=src,
                    dst_ref=dst,
                    send_sem=send_sems.at[part],
                    recv_sem=col_recv.at[n, part],
                    device_id=device,
                    device_id_type=MESH,
                )
                for part, (src, dst) in enumerate(
                    [(src_lat, col_lat[n]), (src_rope, col_rope[n])]
                )
            ]

        def own_copies(at):
            copies = []
            for side, target in enumerate((at - 1, at + 1)):
                if 0 <= target < line:
                    copies += to_line(
                        at,
                        target,
                        pool_lat.at[:, :, core_cols],
                        pool_rope.at[:, core_rope, :],
                        at,
                        own_send.at[side],
                    )
            return copies

        def relay_copies(at, n):
            source = sources[at][n]
            target = at + 1 if source < at else at - 1
            if not 0 <= target < line:
                return []
            return to_line(
                at, target, col_lat[n - 1], col_rope[n - 1], source, relay_send.at[n - 1]
            )

        def arrive(at, n):
            for part, buf in enumerate((col_lat[n - 1], col_rope[n - 1])):
                pltpu.make_async_copy(buf, buf, col_recv.at[n - 1, part]).wait()
            for copy in relay_copies(at, n):
                copy.start()

        def each_place(body):
            for at in range(line):
                pl.when(z == at)(functools.partial(body, at))

        def greet(at):
            near = [t for t in (at - 1, at + 1) if 0 <= t < line]
            for t in near:
                pl.semaphore_signal(
                    barrier, inc=1, device_id=(pool, t * 2 + y, core), device_id_type=MESH
                )
            pl.semaphore_wait(barrier, len(near) + 2)

        barrier = pltpu.get_barrier_semaphore()
        pl.semaphore_signal(barrier, inc=1, device_id=partner, device_id_type=MESH)
        pl.semaphore_signal(barrier, inc=1, device_id=sibling, device_id_type=MESH)
        each_place(greet)
        loads[0].wait()
        table_copy = pltpu.make_async_remote_copy(
            src_ref=table_ref,
            dst_ref=tables_in,
            send_sem=table_send.at[0],
            recv_sem=table_recv.at[0],
            device_id=partner,
            device_id_type=MESH,
        )
        table_copy.start()
        own_table = pltpu.make_async_copy(table_ref, table_smem, local_sem.at[len(pairs)])
        own_table.start()
        loads[1].wait()
        loads[2].wait()

        def send_own(at):
            for copy in own_copies(at):
                copy.start()

        each_place(send_own)
        own_table.wait()
        table_copy.wait_recv()
        partner_table = pltpu.make_async_copy(tables_in, tables_smem, local_sem.at[len(pairs)])
        partner_table.start()
        partner_table.wait()
        own_base = [toks + 2 * n * width for n in range(line)]
        y_base = [toks + (2 * n + 1) * width for n in range(line)]

        def y_copies(n):
            return [
                pltpu.make_async_remote_copy(
                    src_ref=src,
                    dst_ref=dst,
                    send_sem=y_send.at[n, part],
                    recv_sem=y_recv.at[n, part],
                    device_id=partner,
                    device_id_type=MESH,
                )
                for part, (src, dst) in enumerate(
                    [
                        (send_lat.at[n], kv.at[core, pl.ds(y_base[n], width), :]),
                        (send_rope.at[n], kr.at[core_rope, pl.ds(y_base[n], width)]),
                    ]
                )
            ]

        def pack_y(n):
            holder = source_of(n) * 2 + y
            for s in range(slots):
                b = tables_smem[holder, 0, s]
                rows = pl.ds(s * block, block)
                if n == 0:
                    send_lat[n, rows, :] = pool_lat[b, :, core_cols]
                    send_rope[n, :, rows] = pool_rope[b, core_rope, :]
                else:
                    send_lat[n, rows, :] = col_lat[n - 1][b]
                    send_rope[n, :, rows] = col_rope[n - 1][b]
            for copy in y_copies(n):
                copy.start()

        def sibling_copies(n, kind, start):
            lat_rows = kv.at[core, pl.ds(start, width), :]
            rope_rows = kr.at[core_rope, pl.ds(start, width)]
            return [
                pltpu.make_async_remote_copy(
                    src_ref=ref,
                    dst_ref=ref,
                    send_sem=fwd_send.at[n, kind, part],
                    recv_sem=fwd_recv.at[n, kind, part],
                    device_id=sibling,
                    device_id_type=MESH,
                )
                for part, ref in enumerate([lat_rows, rope_rows])
            ]

        def pack_own(n):
            holder = source_of(n) * 2 + y
            for s in range(slots):
                b = table_smem[holder, 0, s]
                rows = pl.ds(own_base[n] + s * block, block)
                kv[core, rows, :] = col_lat[n - 1][b]
                kr[core_rope, rows] = col_rope[n - 1][b]
            copies = sibling_copies(n, 0, own_base[n])
            for copy in copies:
                copy.start()
            return copies

        pack_y(0)
        own_row = me
        places = [(own_base[n], source_of(n) * 2 + y) for n in range(line)]
        places += [(y_base[n], source_of(n) * 2 + 1 - y) for n in range(line)]
    else:
        barrier = pltpu.get_barrier_semaphore()
        for k in order:
            pl.semaphore_signal(barrier, inc=1, device_id=peer(k), device_id_type=MESH)
        pl.semaphore_signal(barrier, inc=1, device_id=sibling, device_id_type=MESH)
        pl.semaphore_wait(barrier, holders)

        loads[0].wait()
        tables = []
        for k in order:
            copy = pltpu.make_async_remote_copy(
                src_ref=table_ref.at[me ^ k],
                dst_ref=table_in.at[k],
                send_sem=table_send.at[k],
                recv_sem=table_recv.at[k],
                device_id=peer(k),
                device_id_type=MESH,
            )
            copy.start()
            tables.append(copy)
        table_in[0] = table_ref[me]
        for copy in tables:
            copy.wait_recv()
        to_smem = pltpu.make_async_copy(table_in, table_smem, local_sem.at[len(pairs)])
        to_smem.start()
        to_smem.wait()

        copies = {}
        loads[1].wait()
        loads[2].wait()
        for k in order:
            for s in range(slots):
                b = table_smem[k, 0, s]
                rows = pl.ds(s * block, block)
                send_lat[k, rows, :] = pool_lat[b, :, pl.ds(pl.multiple_of(core * half, half), half)]
                send_rope[k, :, rows] = pool_rope[
                    b, pl.ds(pl.multiple_of(core * rope_half, rope_half), rope_half), :
                ]
            lat_copy = pltpu.make_async_remote_copy(
                src_ref=send_lat.at[k],
                dst_ref=kv.at[core, pl.ds(base[k], width), :],
                send_sem=lat_send.at[k],
                recv_sem=lat_recv.at[k],
                device_id=peer(k),
                device_id_type=MESH,
            )
            rope_copy = pltpu.make_async_remote_copy(
                src_ref=send_rope.at[k],
                dst_ref=kr.at[
                    pl.ds(pl.multiple_of(core * rope_half, rope_half), rope_half), pl.ds(base[k], width)
                ],
                send_sem=rope_send.at[k],
                recv_sem=rope_recv.at[k],
                device_id=peer(k),
                device_id_type=MESH,
            )
            lat_copy.start()
            rope_copy.start()
            copies[k] = (lat_copy, rope_copy)
        own_row = 0
        places = [(base[k], me ^ k) for k in [0] + order]

    for at in range(3, 9):
        loads[at].wait()
    for c in range(2):
        kv[c, pl.ds(0, toks), :] = span_lat[:, c * half : (c + 1) * half]
    kr[pl.ds(0, rope), pl.ds(0, toks)] = span_rope[...]
    kr[pl.ds(rope, 128 - rope), :] = jnp.zeros((128 - rope, kr.shape[1]), jnp.bfloat16)
    for s in range(slots):
        b = table_smem[own_row, 0, s]
        for c in range(2):
            kv[c, pl.ds(toks + s * block, block), :] = pool_lat[b, :, c * half : (c + 1) * half]
        kr[pl.ds(0, rope), pl.ds(toks + s * block, block)] = pool_rope[b]
    for start, holder in places:
        kr[pl.ds(rope, 16), pl.ds(start, width)] = bias_ref[holder]

    nope32[...] = nope[...].astype(jnp.float32)
    one_col = (lax.broadcasted_iota(jnp.int32, (toks, 128 - rope), 1) == 0).astype(jnp.bfloat16)
    for h in range(heads):
        q_h = nope32[pl.ds(h, toks, stride=heads), :].astype(jnp.bfloat16)
        up = jnp.dot(q_h, key_up[h], preferred_element_type=jnp.float32)
        q_all[pl.ds(h * toks, toks), 0:lat] = (up * scale).astype(jnp.bfloat16)
        rot = rope_q[:, h * rope : (h + 1) * rope].astype(jnp.float32) * scale
        q_all[pl.ds(h * toks, toks), lat:] = jnp.concatenate(
            [rot.astype(jnp.bfloat16), one_col], axis=1
        )

    tile = 8 * toks
    tiles = heads // 8

    def attend(start, size, first):
        keys = pl.ds(start, size)
        for c in range(2):
            kt[c * half : (c + 1) * half, keys] = kv[c, keys, :].T

        def one(t, carry):
            rows = pl.ds(pl.multiple_of(t * tile, tile), tile)
            s = jnp.dot(q_all[rows, :], kt[:, keys], preferred_element_type=jnp.float32)
            if first:
                row = lax.broadcasted_iota(jnp.int32, (tile, size), 0) % toks
                col = lax.broadcasted_iota(jnp.int32, (tile, size), 1)
                s = jnp.where((col <= row) | (col >= toks), s, MASKED)
            top = jnp.max(s, axis=1, keepdims=True)
            if not first:
                old = peak[rows, :]
                top = jnp.maximum(top, old)
                alpha = jnp.exp2(old - top)
            p = jnp.exp2(s - top)
            summed = jnp.sum(p, axis=1, keepdims=True)
            p = p.astype(jnp.bfloat16)
            peak[rows, :] = top
            total[rows, :] = summed if first else total[rows, :] * alpha + summed
            for c in range(2):
                cols = pl.ds(c * half, half)
                mixed = jnp.dot(p, kv[c, keys, :], preferred_element_type=jnp.float32)
                acc[rows, cols] = mixed if first else acc[rows, cols] * alpha + mixed
            return carry

        lax.fori_loop(0, tiles, one, 0)

    attend(0, toks + width, True)

    if line:
        forwards = []

        def take_y(n):
            for copy in y_copies(n):
                copy.wait_recv()
            copies = sibling_copies(n, 1, y_base[n])
            for copy in copies:
                copy.start()
            return copies

        for n in range(1, line):

            def arrivals(at, n=n):
                inner = 0 < at < line - 1
                ahead = [n] if not inner else [1, 2] if n == 1 else [n + 1]
                for m in ahead:
                    if m < line:
                        arrive(at, m)

            each_place(arrivals)
            pack_y(n)
            current = pack_own(n) + take_y(n - 1)
            for copy in current:
                copy.wait_recv()
            forwards += current
            attend(y_base[n - 1], 2 * width, False)
        current = take_y(line - 1)
        for copy in current:
            copy.wait_recv()
        forwards += current
        attend(y_base[line - 1], width, False)
    else:
        forwards = []
        group = max(1, 768 // width)
        for at in range(0, len(order), group):
            members = order[at : at + group]
            current = []
            for k in members:
                copies[k][0].wait_recv()
                copies[k][1].wait_recv()
                lat_rows = kv.at[core, pl.ds(base[k], width), :]
                rope_rows = kr.at[
                    pl.ds(pl.multiple_of(core * rope_half, rope_half), rope_half), pl.ds(base[k], width)
                ]
                lat_fwd = pltpu.make_async_remote_copy(
                    src_ref=lat_rows,
                    dst_ref=lat_rows,
                    send_sem=fwd_lat_send.at[k],
                    recv_sem=fwd_lat_recv.at[k],
                    device_id=sibling,
                    device_id_type=MESH,
                )
                rope_fwd = pltpu.make_async_remote_copy(
                    src_ref=rope_rows,
                    dst_ref=rope_rows,
                    send_sem=fwd_rope_send.at[k],
                    recv_sem=fwd_rope_recv.at[k],
                    device_id=sibling,
                    device_id_type=MESH,
                )
                lat_fwd.start()
                rope_fwd.start()
                current += [lat_fwd, rope_fwd]
            for copy in current:
                copy.wait_recv()
            forwards += current
            attend(base[members[0]], len(members) * width, False)

    loads[9].wait()
    live = lax.broadcasted_iota(jnp.int32, (toks, value_up.shape[2]), 0) < count_ref[0]
    for h in range(heads):
        rows = pl.ds(h * toks, toks)
        mixed = (acc[rows, :] / total[rows, :]).astype(jnp.bfloat16)
        up = jnp.dot(mixed, value_up[h], preferred_element_type=jnp.float32)
        vdim = value_up.shape[2]
        out_ref[:, h * vdim : (h + 1) * vdim] = jnp.where(live, up, 0.0).astype(out_ref.dtype)

    if line:

        def drain(at):
            for copy in own_copies(at):
                copy.wait_send()
            for n in range(1, line):
                for copy in relay_copies(at, n):
                    copy.wait_send()

        each_place(drain)
        table_copy.wait_send()
        for n in range(line):
            for copy in y_copies(n):
                copy.wait_send()
        for copy in forwards:
            copy.wait_send()
    else:
        for copy in tables + forwards:
            copy.wait_send()
        for k in order:
            copies[k][0].wait_send()
            copies[k][1].wait_send()


def on_device(
    query_nope,
    query_rope,
    key_up,
    value_up,
    span_latent,
    span_rope,
    pool_latent,
    pool_rope,
    hit_holders,
    hit_blocks,
    prefix_len,
    span_len,
):
    holders = lax.axis_size("hold")
    toks, heads, nope_width = query_nope.shape
    lat = key_up.shape[2]
    rope = span_rope.shape[0]
    block = pool_latent.shape[1]
    list_len = hit_holders.shape[1]
    vdim = value_up.shape[2]
    slots = (list_len + holders - 1) // holders
    width = slots * block
    scale = float(nope_width + rope) ** (-0.5) * math.log2(math.e)

    row = hit_holders[0]
    entry = jnp.arange(list_len)
    rank = jnp.sum((row[:, None] == row[None, :]) & (entry[None, :] < entry[:, None]), axis=1)
    match = (row[None, None, :] == jnp.arange(holders)[:, None, None]) & (
        rank[None, None, :] == jnp.arange(slots)[None, :, None]
    )
    ids = jnp.sum(jnp.where(match, hit_blocks[0][None, None, :], 0), axis=2)
    table = jnp.broadcast_to(
        jnp.pad(ids, ((0, 0), (0, 128 - slots)))[:, None, :], (holders, 8, 128)
    ).astype(jnp.int32)
    seen = jnp.sum(jnp.where(match, jnp.maximum(prefix_len[0] - entry * block, 0), 0), axis=2)
    hidden = jnp.arange(block)[None, None, :] >= seen[:, :, None]
    bias = jnp.where(hidden, MASKED, 0.0).reshape(holders, 1, width)
    first_row = jnp.arange(16)[None, :, None] == 0
    bias = jnp.where(first_row, bias, 0.0).astype(jnp.bfloat16)

    keys = toks + holders * width
    rows = heads * toks
    vmem = pl.BlockSpec(memory_space=pltpu.VMEM)
    any_space = pl.BlockSpec(memory_space=pl.ANY)
    sems = pltpu.SemaphoreType.DMA((holders,))
    line = holders // 2 if holders <= 8 else 0
    line_scratch = []
    if line:
        stored = pool_latent.shape[0]
        line_scratch = [pltpu.VMEM((stored, block, lat // 2), jnp.bfloat16)] * (line - 1)
        line_scratch += [pltpu.VMEM((stored, rope // 2, block), jnp.bfloat16)] * (line - 1)
        line_scratch += [
            pltpu.VMEM(table.shape, jnp.int32),
            pltpu.SMEM(table.shape, jnp.int32),
            pltpu.SemaphoreType.DMA((2, 2)),
            pltpu.SemaphoreType.DMA((line, 2)),
            pltpu.SemaphoreType.DMA((line, 2)),
            pltpu.SemaphoreType.DMA((line, 2)),
            pltpu.SemaphoreType.DMA((line, 2)),
            pltpu.SemaphoreType.DMA((line, 2, 2)),
            pltpu.SemaphoreType.DMA((line, 2, 2)),
        ]
    sizes = (holders, slots, heads, toks, block, lat, rope, scale, line)
    return pl.pallas_call(
        functools.partial(kernel, sizes),
        out_shape=jax.ShapeDtypeStruct((toks, heads * vdim), jnp.bfloat16),
        in_specs=[any_space] * 2 + [pl.BlockSpec(memory_space=pltpu.SMEM)] + [any_space] * 8,
        out_specs=vmem,
        scratch_shapes=[
            pltpu.VMEM(table.shape, jnp.int32),
            pltpu.VMEM(bias.shape, jnp.bfloat16),
            pltpu.VMEM(pool_latent.shape, jnp.bfloat16),
            pltpu.VMEM(pool_rope.shape, jnp.bfloat16),
            pltpu.VMEM(span_latent.shape, jnp.bfloat16),
            pltpu.VMEM(span_rope.shape, jnp.bfloat16),
            pltpu.VMEM(query_rope.shape, jnp.bfloat16),
            pltpu.VMEM((holders, 8, 128), jnp.int32),
            pltpu.SMEM((holders, 8, 128), jnp.int32),
            pltpu.VMEM((holders, width, lat // 2), jnp.bfloat16),
            pltpu.VMEM((holders, rope // 2, width), jnp.bfloat16),
            pltpu.VMEM((2, keys, lat // 2), jnp.bfloat16),
            pltpu.VMEM((lat + 128, keys), jnp.bfloat16),
            pltpu.VMEM((rows, nope_width), jnp.bfloat16),
            pltpu.VMEM((rows, nope_width), jnp.float32),
            pltpu.VMEM(key_up.shape, jnp.bfloat16),
            pltpu.VMEM(value_up.shape, jnp.bfloat16),
            pltpu.VMEM((rows, lat + 128), jnp.bfloat16),
            pltpu.VMEM((rows, lat), jnp.float32),
            pltpu.VMEM((rows, 1), jnp.float32),
            pltpu.VMEM((rows, 1), jnp.float32),
            pltpu.SemaphoreType.DMA((11,)),
        ]
        + [sems] * 10
        + line_scratch,
        compiler_params=pltpu.CompilerParams(
            collective_id=0, has_side_effects=True, vmem_limit_bytes=56 * 1024 * 1024
        ),
    )(
        table,
        bias,
        span_len,
        pool_latent,
        pool_rope,
        span_latent,
        span_rope,
        query_nope.reshape(rows, nope_width),
        query_rope,
        key_up,
        value_up,
    )


def solution(mesh):
    return jax.shard_map(
        on_device,
        mesh=mesh,
        in_specs=(
            P(("pool", "hold"), "head", None),
            P(("pool", "hold"), "head"),
            P("head", None, None),
            P("head", None, None),
            P(("pool", "hold"), None),
            P(None, ("pool", "hold")),
            P(("pool", "hold"), None, None),
            P(("pool", "hold"), None, None),
            P(("pool", "hold"), None),
            P(("pool", "hold"), None),
            P(("pool", "hold")),
            P(("pool", "hold")),
        ),
        out_specs=P(("pool", "hold"), "head"),
        check_vma=False,
    )
```

```python
import functools
import math

import jax
import jax.numpy as jnp
from jax import lax
from jax.experimental import pallas as pl
from jax.experimental.pallas import tpu as pltpu
from jax.sharding import PartitionSpec as P

MESH = pl.DeviceIdType.MESH
MASKED = -1e30


def send_order(holders):
    near = list(range(1, holders // 2))
    far = list(range(holders // 2, holders))
    order = []
    while near or far:
        if near:
            order.append(near.pop(0))
        if far:
            order.append(far.pop(0))
    return order


def kernel(
    sizes,
    hit_scalars,
    prefix_ref,
    count_ref,
    holders_hbm,
    blocks_hbm,
    pool_lat_hbm,
    pool_rope_hbm,
    span_lat_hbm,
    span_rope_hbm,
    nope_hbm,
    rope_q_hbm,
    key_up_hbm,
    value_up_hbm,
    out_ref,
    table_ref,
    bias_ref,
    holders_ref,
    blocks_ref,
    pool_lat,
    pool_rope,
    span_lat,
    span_rope,
    rope_q,
    table_in,
    table_smem,
    send_lat,
    send_rope,
    kv,
    kt,
    nope,
    nope32,
    key_up,
    value_up,
    q_all,
    acc,
    peak,
    total,
    local_sem,
    table_send,
    table_recv,
    lat_send,
    lat_recv,
    rope_send,
    rope_recv,
    fwd_lat_send,
    fwd_lat_recv,
    fwd_rope_send,
    fwd_rope_recv,
    *line_refs,
):
    holders, slots, heads, toks, block, lat, rope, scale, line = sizes
    width = slots * block
    half = lat // 2
    rope_half = rope // 2
    pool, me, core = lax.axis_index("pool"), lax.axis_index("hold"), lax.axis_index("head")
    other = 1 - core
    sibling = (pool, me, other)
    kr = kt.at[pl.ds(lat, 128), :]
    order = send_order(holders)
    base = {0: toks}
    for at, k in enumerate(order):
        base[k] = toks + (at + 1) * width

    def peer(k):
        return (pool, me ^ k, core)

    pairs = [
        (pool_lat_hbm, pool_lat),
        (pool_rope_hbm, pool_rope),
        (span_lat_hbm, span_lat),
        (span_rope_hbm, span_rope),
        (nope_hbm, nope),
        (key_up_hbm, key_up),
        (rope_q_hbm, rope_q),
        (value_up_hbm, value_up),
        (holders_hbm, holders_ref),
        (blocks_hbm, blocks_ref),
    ]
    loads = []
    for at, (src, dst) in enumerate(pairs):
        load = pltpu.make_async_copy(src, dst, local_sem.at[at])
        load.start()
        loads.append(load)

    def make_tables():
        loads[8].wait()
        loads[9].wait()
        list_len = holders_ref.shape[1]
        hit_row, block_row = holders_ref[...], blocks_ref[...]
        entry = lax.broadcasted_iota(jnp.int32, (1, list_len), 1)
        rank = jnp.zeros((1, list_len), jnp.int32)
        for j in range(list_len):
            rank += jnp.where((hit_row == hit_scalars[0, j]) & (entry > j), 1, 0)
        left = jnp.maximum(prefix_ref[0] - entry * block, 0)
        holder = lax.broadcasted_iota(jnp.int32, (holders, list_len), 0)
        place = lax.broadcasted_iota(jnp.int32, (holders, 128), 1)
        token = lax.broadcasted_iota(jnp.int32, (holders, block), 1)
        ids = jnp.zeros((holders, 128), jnp.int32)
        for s in range(slots):
            match = (hit_row == holder) & (rank == s)
            picked = jnp.sum(jnp.where(match, block_row, 0), axis=1, keepdims=True)
            seen = jnp.sum(jnp.where(match, left, 0), axis=1, keepdims=True)
            ids = jnp.where(place == s, picked, ids)
            bias_ref[:, s * block : (s + 1) * block] = jnp.where(token >= seen, MASKED, 0.0)
        for h in range(holders):
            table_ref[h] = jnp.broadcast_to(ids[h : h + 1, :], (8, 128))

    if line:
        z, y = me // 2, me % 2
        partner = (pool, me ^ 1, core)
        col_lat, col_rope = line_refs[: line - 1], line_refs[line - 1 : 2 * (line - 1)]
        (tables_in, tables_smem, own_send, relay_send, col_recv, y_send, y_recv, fwd_send, fwd_recv) = (
            line_refs[2 * (line - 1) :]
        )
        sources = [sorted(range(line), key=lambda s, at=at: (abs(s - at), s)) for at in range(line)]
        core_cols = pl.ds(pl.multiple_of(core * half, half), half)
        core_rope = pl.ds(pl.multiple_of(core * rope_half, rope_half), rope_half)

        def source_of(n):
            code = sum(sources[at][n] << (4 * at) for at in range(line))
            return (code >> (4 * z)) & 15

        def to_line(at, target, src_lat, src_rope, source, send_sems):
            n = sources[target].index(source) - 1
            device = (pool, target * 2 + y, core)
            return [
                pltpu.make_async_remote_copy(
                    src_ref=src,
                    dst_ref=dst,
                    send_sem=send_sems.at[part],
                    recv_sem=col_recv.at[n, part],
                    device_id=device,
                    device_id_type=MESH,
                )
                for part, (src, dst) in enumerate(
                    [(src_lat, col_lat[n]), (src_rope, col_rope[n])]
                )
            ]

        def own_copies(at):
            copies = []
            for side, target in enumerate((at - 1, at + 1)):
                if 0 <= target < line:
                    copies += to_line(
                        at,
                        target,
                        pool_lat.at[:, :, core_cols],
                        pool_rope.at[:, core_rope, :],
                        at,
                        own_send.at[side],
                    )
            return copies

        def relay_copies(at, n):
            source = sources[at][n]
            target = at + 1 if source < at else at - 1
            if not 0 <= target < line:
                return []
            return to_line(
                at, target, col_lat[n - 1], col_rope[n - 1], source, relay_send.at[n - 1]
            )

        def arrive(at, n):
            for part, buf in enumerate((col_lat[n - 1], col_rope[n - 1])):
                pltpu.make_async_copy(buf, buf, col_recv.at[n - 1, part]).wait()
            for copy in relay_copies(at, n):
                copy.start()

        def each_place(body):
            for at in range(line):
                pl.when(z == at)(functools.partial(body, at))

        def greet(at):
            near = [t for t in (at - 1, at + 1) if 0 <= t < line]
            for t in near:
                pl.semaphore_signal(
                    barrier, inc=1, device_id=(pool, t * 2 + y, core), device_id_type=MESH
                )
            pl.semaphore_wait(barrier, len(near) + 2)

        barrier = pltpu.get_barrier_semaphore()
        pl.semaphore_signal(barrier, inc=1, device_id=partner, device_id_type=MESH)
        pl.semaphore_signal(barrier, inc=1, device_id=sibling, device_id_type=MESH)
        make_tables()
        each_place(greet)
        table_copy = pltpu.make_async_remote_copy(
            src_ref=table_ref,
            dst_ref=tables_in,
            send_sem=table_send.at[0],
            recv_sem=table_recv.at[0],
            device_id=partner,
            device_id_type=MESH,
        )
        table_copy.start()
        own_table = pltpu.make_async_copy(table_ref, table_smem, local_sem.at[len(pairs)])
        own_table.start()
        loads[0].wait()
        loads[1].wait()

        def send_own(at):
            for copy in own_copies(at):
                copy.start()

        each_place(send_own)
        own_table.wait()
        table_copy.wait_recv()
        partner_table = pltpu.make_async_copy(tables_in, tables_smem, local_sem.at[len(pairs)])
        partner_table.start()
        partner_table.wait()
        own_base = [toks + 2 * n * width for n in range(line)]
        y_base = [toks + (2 * n + 1) * width for n in range(line)]

        def y_copies(n):
            return [
                pltpu.make_async_remote_copy(
                    src_ref=src,
                    dst_ref=dst,
                    send_sem=y_send.at[n, part],
                    recv_sem=y_recv.at[n, part],
                    device_id=partner,
                    device_id_type=MESH,
                )
                for part, (src, dst) in enumerate(
                    [
                        (send_lat.at[n], kv.at[core, pl.ds(y_base[n], width), :]),
                        (send_rope.at[n], kr.at[core_rope, pl.ds(y_base[n], width)]),
                    ]
                )
            ]

        def pack_y(n):
            holder = source_of(n) * 2 + y
            for s in range(slots):
                b = tables_smem[holder, 0, s]
                rows = pl.ds(s * block, block)
                if n == 0:
                    send_lat[n, rows, :] = pool_lat[b, :, core_cols]
                    send_rope[n, :, rows] = pool_rope[b, core_rope, :]
                else:
                    send_lat[n, rows, :] = col_lat[n - 1][b]
                    send_rope[n, :, rows] = col_rope[n - 1][b]
            for copy in y_copies(n):
                copy.start()

        def sibling_copies(n, kind, start):
            lat_rows = kv.at[core, pl.ds(start, width), :]
            rope_rows = kr.at[core_rope, pl.ds(start, width)]
            return [
                pltpu.make_async_remote_copy(
                    src_ref=ref,
                    dst_ref=ref,
                    send_sem=fwd_send.at[n, kind, part],
                    recv_sem=fwd_recv.at[n, kind, part],
                    device_id=sibling,
                    device_id_type=MESH,
                )
                for part, ref in enumerate([lat_rows, rope_rows])
            ]

        def pack_own(n):
            holder = source_of(n) * 2 + y
            for s in range(slots):
                b = table_smem[holder, 0, s]
                rows = pl.ds(own_base[n] + s * block, block)
                kv[core, rows, :] = col_lat[n - 1][b]
                kr[core_rope, rows] = col_rope[n - 1][b]
            copies = sibling_copies(n, 0, own_base[n])
            for copy in copies:
                copy.start()
            return copies

        pack_y(0)
        own_row = me
        places = [(own_base[n], source_of(n) * 2 + y) for n in range(line)]
        places += [(y_base[n], source_of(n) * 2 + 1 - y) for n in range(line)]
    else:
        barrier = pltpu.get_barrier_semaphore()
        for k in order:
            pl.semaphore_signal(barrier, inc=1, device_id=peer(k), device_id_type=MESH)
        pl.semaphore_signal(barrier, inc=1, device_id=sibling, device_id_type=MESH)
        make_tables()
        pl.semaphore_wait(barrier, holders)

        tables = []
        for k in order:
            copy = pltpu.make_async_remote_copy(
                src_ref=table_ref.at[me ^ k],
                dst_ref=table_in.at[k],
                send_sem=table_send.at[k],
                recv_sem=table_recv.at[k],
                device_id=peer(k),
                device_id_type=MESH,
            )
            copy.start()
            tables.append(copy)
        table_in[0] = table_ref[me]
        for copy in tables:
            copy.wait_recv()
        to_smem = pltpu.make_async_copy(table_in, table_smem, local_sem.at[len(pairs)])
        to_smem.start()
        to_smem.wait()

        copies = {}
        loads[0].wait()
        loads[1].wait()
        for k in order:
            for s in range(slots):
                b = table_smem[k, 0, s]
                rows = pl.ds(s * block, block)
                send_lat[k, rows, :] = pool_lat[b, :, pl.ds(pl.multiple_of(core * half, half), half)]
                send_rope[k, :, rows] = pool_rope[
                    b, pl.ds(pl.multiple_of(core * rope_half, rope_half), rope_half), :
                ]
            lat_copy = pltpu.make_async_remote_copy(
                src_ref=send_lat.at[k],
                dst_ref=kv.at[core, pl.ds(base[k], width), :],
                send_sem=lat_send.at[k],
                recv_sem=lat_recv.at[k],
                device_id=peer(k),
                device_id_type=MESH,
            )
            rope_copy = pltpu.make_async_remote_copy(
                src_ref=send_rope.at[k],
                dst_ref=kr.at[
                    pl.ds(pl.multiple_of(core * rope_half, rope_half), rope_half), pl.ds(base[k], width)
                ],
                send_sem=rope_send.at[k],
                recv_sem=rope_recv.at[k],
                device_id=peer(k),
                device_id_type=MESH,
            )
            lat_copy.start()
            rope_copy.start()
            copies[k] = (lat_copy, rope_copy)
        own_row = 0
        places = [(base[k], me ^ k) for k in [0] + order]

    for at in range(2, 7):
        loads[at].wait()
    for c in range(2):
        kv[c, pl.ds(0, toks), :] = span_lat[:, c * half : (c + 1) * half]
    kr[pl.ds(0, rope), pl.ds(0, toks)] = span_rope[...]
    kr[pl.ds(rope, 128 - rope), :] = jnp.zeros((128 - rope, kr.shape[1]), jnp.bfloat16)
    for s in range(slots):
        b = table_smem[own_row, 0, s]
        for c in range(2):
            kv[c, pl.ds(toks + s * block, block), :] = pool_lat[b, :, c * half : (c + 1) * half]
        kr[pl.ds(0, rope), pl.ds(toks + s * block, block)] = pool_rope[b]
    top_row = lax.broadcasted_iota(jnp.int32, (16, width), 0) == 0
    for start, holder in places:
        row = bias_ref[pl.ds(holder, 1), :]
        kr[pl.ds(rope, 16), pl.ds(start, width)] = jnp.where(top_row, row, 0.0).astype(jnp.bfloat16)

    nope32[...] = nope[...].astype(jnp.float32)
    one_col = (lax.broadcasted_iota(jnp.int32, (toks, 128 - rope), 1) == 0).astype(jnp.bfloat16)
    for h in range(heads):
        q_h = nope32[pl.ds(h, toks, stride=heads), :].astype(jnp.bfloat16)
        up = jnp.dot(q_h, key_up[h], preferred_element_type=jnp.float32)
        q_all[pl.ds(h * toks, toks), 0:lat] = (up * scale).astype(jnp.bfloat16)
        rot = rope_q[:, h * rope : (h + 1) * rope].astype(jnp.float32) * scale
        q_all[pl.ds(h * toks, toks), lat:] = jnp.concatenate(
            [rot.astype(jnp.bfloat16), one_col], axis=1
        )

    tile = 16 * toks
    part = 2 * toks
    tiles = heads // 16

    def attend(start, size, first):
        keys = pl.ds(start, size)
        for c in range(2):
            kt[c * half : (c + 1) * half, keys] = kv[c, keys, :].T

        def one(t, carry):
            parts = [
                pl.ds(pl.multiple_of(t * tile + at * part, part), part) for at in range(tile // part)
            ]
            scores = [
                jnp.dot(q_all[rows, :], kt[:, keys], preferred_element_type=jnp.float32)
                for rows in parts
            ]
            if first:
                row = lax.broadcasted_iota(jnp.int32, (part, size), 0) % toks
                col = lax.broadcasted_iota(jnp.int32, (part, size), 1)
                seen = (col <= row) | (col >= toks)
                scores = [jnp.where(seen, s, MASKED) for s in scores]
            else:
                old = [peak[rows, :] for rows in parts]
                old_total = [total[rows, :] for rows in parts]
            tops, probs, sums, alphas = [], [], [], []
            for at, s in enumerate(scores):
                top = jnp.max(s, axis=1, keepdims=True)
                if not first:
                    top = jnp.maximum(top, old[at])
                    alphas.append(jnp.exp2(old[at] - top))
                p = jnp.exp2(s - top)
                tops.append(top)
                sums.append(jnp.sum(p, axis=1, keepdims=True))
                probs.append(p.astype(jnp.bfloat16))
            mixed = [
                [jnp.dot(p, kv[c, keys, :], preferred_element_type=jnp.float32) for c in range(2)]
                for p in probs
            ]
            for at, rows in enumerate(parts):
                peak[rows, :] = tops[at]
                total[rows, :] = sums[at] if first else old_total[at] * alphas[at] + sums[at]
                for c in range(2):
                    cols = pl.ds(c * half, half)
                    if first:
                        acc[rows, cols] = mixed[at][c]
                    else:
                        acc[rows, cols] = acc[rows, cols] * alphas[at] + mixed[at][c]
            return carry

        lax.fori_loop(0, tiles, one, 0)

    attend(0, toks + width, True)

    if line:
        forwards = []

        def take_y(n):
            for copy in y_copies(n):
                copy.wait_recv()
            copies = sibling_copies(n, 1, y_base[n])
            for copy in copies:
                copy.start()
            return copies

        for n in range(1, line):

            def arrivals(at, n=n):
                inner = 0 < at < line - 1
                ahead = [n] if not inner else [1, 2] if n == 1 else [n + 1]
                for m in ahead:
                    if m < line:
                        arrive(at, m)

            each_place(arrivals)
            pack_y(n)
            current = pack_own(n) + take_y(n - 1)
            for copy in current:
                copy.wait_recv()
            forwards += current
            attend(y_base[n - 1], 2 * width, False)
        current = take_y(line - 1)
        for copy in current:
            copy.wait_recv()
        forwards += current
        attend(y_base[line - 1], width, False)
    else:
        forwards = []
        group = max(1, 768 // width)
        for at in range(0, len(order), group):
            members = order[at : at + group]
            current = []
            for k in members:
                copies[k][0].wait_recv()
                copies[k][1].wait_recv()
                lat_rows = kv.at[core, pl.ds(base[k], width), :]
                rope_rows = kr.at[
                    pl.ds(pl.multiple_of(core * rope_half, rope_half), rope_half), pl.ds(base[k], width)
                ]
                lat_fwd = pltpu.make_async_remote_copy(
                    src_ref=lat_rows,
                    dst_ref=lat_rows,
                    send_sem=fwd_lat_send.at[k],
                    recv_sem=fwd_lat_recv.at[k],
                    device_id=sibling,
                    device_id_type=MESH,
                )
                rope_fwd = pltpu.make_async_remote_copy(
                    src_ref=rope_rows,
                    dst_ref=rope_rows,
                    send_sem=fwd_rope_send.at[k],
                    recv_sem=fwd_rope_recv.at[k],
                    device_id=sibling,
                    device_id_type=MESH,
                )
                lat_fwd.start()
                rope_fwd.start()
                current += [lat_fwd, rope_fwd]
            for copy in current:
                copy.wait_recv()
            forwards += current
            attend(base[members[0]], len(members) * width, False)

    loads[7].wait()
    live = lax.broadcasted_iota(jnp.int32, (toks, value_up.shape[2]), 0) < count_ref[0]
    for h in range(heads):
        rows = pl.ds(h * toks, toks)
        mixed = (acc[rows, :] * (1.0 / total[rows, :])).astype(jnp.bfloat16)
        up = jnp.dot(mixed, value_up[h], preferred_element_type=jnp.float32)
        vdim = value_up.shape[2]
        out_ref[:, h * vdim : (h + 1) * vdim] = jnp.where(live, up, 0.0).astype(out_ref.dtype)

    if line:

        def drain(at):
            for copy in own_copies(at):
                copy.wait_send()
            for n in range(1, line):
                for copy in relay_copies(at, n):
                    copy.wait_send()

        each_place(drain)
        table_copy.wait_send()
        for n in range(line):
            for copy in y_copies(n):
                copy.wait_send()
        for copy in forwards:
            copy.wait_send()
    else:
        for copy in tables + forwards:
            copy.wait_send()
        for k in order:
            copies[k][0].wait_send()
            copies[k][1].wait_send()


def on_device(
    query_nope,
    query_rope,
    key_up,
    value_up,
    span_latent,
    span_rope,
    pool_latent,
    pool_rope,
    hit_holders,
    hit_blocks,
    prefix_len,
    span_len,
):
    holders = lax.axis_size("hold")
    toks, heads, nope_width = query_nope.shape
    lat = key_up.shape[2]
    rope = span_rope.shape[0]
    block = pool_latent.shape[1]
    list_len = hit_holders.shape[1]
    vdim = value_up.shape[2]
    slots = (list_len + holders - 1) // holders
    width = slots * block
    scale = float(nope_width + rope) ** (-0.5) * math.log2(math.e)

    keys = toks + holders * width
    rows = heads * toks
    vmem = pl.BlockSpec(memory_space=pltpu.VMEM)
    any_space = pl.BlockSpec(memory_space=pl.ANY)
    sems = pltpu.SemaphoreType.DMA((holders,))
    line = holders // 2 if holders <= 8 else 0
    line_scratch = []
    if line:
        stored = pool_latent.shape[0]
        line_scratch = [pltpu.VMEM((stored, block, lat // 2), jnp.bfloat16)] * (line - 1)
        line_scratch += [pltpu.VMEM((stored, rope // 2, block), jnp.bfloat16)] * (line - 1)
        line_scratch += [
            pltpu.VMEM((holders, 8, 128), jnp.int32),
            pltpu.SMEM((holders, 8, 128), jnp.int32),
            pltpu.SemaphoreType.DMA((2, 2)),
            pltpu.SemaphoreType.DMA((line, 2)),
            pltpu.SemaphoreType.DMA((line, 2)),
            pltpu.SemaphoreType.DMA((line, 2)),
            pltpu.SemaphoreType.DMA((line, 2)),
            pltpu.SemaphoreType.DMA((line, 2, 2)),
            pltpu.SemaphoreType.DMA((line, 2, 2)),
        ]
    sizes = (holders, slots, heads, toks, block, lat, rope, scale, line)
    return pl.pallas_call(
        functools.partial(kernel, sizes),
        out_shape=jax.ShapeDtypeStruct((toks, heads * vdim), jnp.bfloat16),
        in_specs=[pl.BlockSpec(memory_space=pltpu.SMEM)] * 3 + [any_space] * 10,
        out_specs=vmem,
        scratch_shapes=[
            pltpu.VMEM((holders, 8, 128), jnp.int32),
            pltpu.VMEM((holders, width), jnp.float32),
            pltpu.VMEM(hit_holders.shape, jnp.int32),
            pltpu.VMEM(hit_blocks.shape, jnp.int32),
            pltpu.VMEM(pool_latent.shape, jnp.bfloat16),
            pltpu.VMEM(pool_rope.shape, jnp.bfloat16),
            pltpu.VMEM(span_latent.shape, jnp.bfloat16),
            pltpu.VMEM(span_rope.shape, jnp.bfloat16),
            pltpu.VMEM(query_rope.shape, jnp.bfloat16),
            pltpu.VMEM((holders, 8, 128), jnp.int32),
            pltpu.SMEM((holders, 8, 128), jnp.int32),
            pltpu.VMEM((holders, width, lat // 2), jnp.bfloat16),
            pltpu.VMEM((holders, rope // 2, width), jnp.bfloat16),
            pltpu.VMEM((2, keys, lat // 2), jnp.bfloat16),
            pltpu.VMEM((lat + 128, keys), jnp.bfloat16),
            pltpu.VMEM((rows, nope_width), jnp.bfloat16),
            pltpu.VMEM((rows, nope_width), jnp.float32),
            pltpu.VMEM(key_up.shape, jnp.bfloat16),
            pltpu.VMEM(value_up.shape, jnp.bfloat16),
            pltpu.VMEM((rows, lat + 128), jnp.bfloat16),
            pltpu.VMEM((rows, lat), jnp.float32),
            pltpu.VMEM((rows, 1), jnp.float32),
            pltpu.VMEM((rows, 1), jnp.float32),
            pltpu.SemaphoreType.DMA((11,)),
        ]
        + [sems] * 10
        + line_scratch,
        compiler_params=pltpu.CompilerParams(
            collective_id=0, has_side_effects=True, vmem_limit_bytes=56 * 1024 * 1024
        ),
    )(
        hit_holders,
        prefix_len,
        span_len,
        hit_holders,
        hit_blocks,
        pool_latent,
        pool_rope,
        span_latent,
        span_rope,
        query_nope.reshape(rows, nope_width),
        query_rope,
        key_up,
        value_up,
    )


def solution(mesh):
    return jax.shard_map(
        on_device,
        mesh=mesh,
        in_specs=(
            P(("pool", "hold"), "head", None),
            P(("pool", "hold"), "head"),
            P("head", None, None),
            P("head", None, None),
            P(("pool", "hold"), None),
            P(None, ("pool", "hold")),
            P(("pool", "hold"), None, None),
            P(("pool", "hold"), None, None),
            P(("pool", "hold"), None),
            P(("pool", "hold"), None),
            P(("pool", "hold")),
            P(("pool", "hold")),
        ),
        out_specs=P(("pool", "hold"), "head"),
        check_vma=False,
    )
```

```python
import functools
import math

import jax
import jax.numpy as jnp
from jax import lax
from jax.experimental import pallas as pl
from jax.experimental.pallas import tpu as pltpu
from jax.sharding import PartitionSpec as P

MESH = pl.DeviceIdType.MESH
MASKED = -1e30


def send_order(holders):
    near = list(range(1, holders // 2))
    far = list(range(holders // 2, holders))
    order = []
    while near or far:
        if near:
            order.append(near.pop(0))
        if far:
            order.append(far.pop(0))
    return order


def kernel(
    sizes,
    hit_scalars,
    prefix_ref,
    count_ref,
    holders_hbm,
    blocks_hbm,
    pool_lat_hbm,
    pool_rope_hbm,
    span_lat_hbm,
    span_rope_hbm,
    nope_hbm,
    rope_q_hbm,
    key_up_hbm,
    value_up_hbm,
    out_ref,
    table_ref,
    bias_ref,
    holders_ref,
    blocks_ref,
    pool_lat,
    pool_rope,
    span_lat,
    span_rope,
    rope_q,
    table_in,
    table_smem,
    send_lat,
    send_rope,
    kv,
    kt,
    nope,
    nope32,
    key_up,
    value_up,
    q_all,
    acc,
    peak,
    total,
    local_sem,
    table_send,
    table_recv,
    lat_send,
    lat_recv,
    rope_send,
    rope_recv,
    fwd_lat_send,
    fwd_lat_recv,
    fwd_rope_send,
    fwd_rope_recv,
    *line_refs,
):
    holders, slots, heads, toks, block, lat, rope, scale, line = sizes
    width = slots * block
    half = lat // 2
    rope_half = rope // 2
    pool, me, core = lax.axis_index("pool"), lax.axis_index("hold"), lax.axis_index("head")
    other = 1 - core
    sibling = (pool, me, other)
    kr = kt.at[pl.ds(lat, 128), :]
    order = send_order(holders)
    base = {0: toks}
    for at, k in enumerate(order):
        base[k] = toks + (at + 1) * width

    def peer(k):
        return (pool, me ^ k, core)

    pairs = [
        (pool_lat_hbm, pool_lat),
        (pool_rope_hbm, pool_rope),
        (span_lat_hbm, span_lat),
        (span_rope_hbm, span_rope),
        (nope_hbm, nope),
        (key_up_hbm, key_up),
        (rope_q_hbm, rope_q),
        (value_up_hbm, value_up),
        (holders_hbm, holders_ref),
        (blocks_hbm, blocks_ref),
    ]
    loads = []
    for at, (src, dst) in enumerate(pairs):
        load = pltpu.make_async_copy(src, dst, local_sem.at[at])
        load.start()
        loads.append(load)

    def make_tables():
        loads[8].wait()
        loads[9].wait()
        list_len = holders_ref.shape[1]
        hit_row, block_row = holders_ref[...], blocks_ref[...]
        entry = lax.broadcasted_iota(jnp.int32, (1, list_len), 1)
        rank = jnp.zeros((1, list_len), jnp.int32)
        for j in range(list_len):
            rank += jnp.where((hit_row == hit_scalars[0, j]) & (entry > j), 1, 0)
        left = jnp.maximum(prefix_ref[0] - entry * block, 0)
        holder = lax.broadcasted_iota(jnp.int32, (holders, list_len), 0)
        place = lax.broadcasted_iota(jnp.int32, (holders, 128), 1)
        token = lax.broadcasted_iota(jnp.int32, (holders, block), 1)
        ids = jnp.zeros((holders, 128), jnp.int32)
        for s in range(slots):
            match = (hit_row == holder) & (rank == s)
            picked = jnp.sum(jnp.where(match, block_row, 0), axis=1, keepdims=True)
            seen = jnp.sum(jnp.where(match, left, 0), axis=1, keepdims=True)
            ids = jnp.where(place == s, picked, ids)
            bias_ref[:, s * block : (s + 1) * block] = jnp.where(token >= seen, MASKED, 0.0)
        for h in range(holders):
            table_ref[h] = jnp.broadcast_to(ids[h : h + 1, :], (8, 128))

    if line:
        z, y = me // 2, me % 2
        partner = (pool, me ^ 1, core)
        col_lat, col_rope = line_refs[: line - 1], line_refs[line - 1 : 2 * (line - 1)]
        (tables_in, tables_smem, own_send, relay_send, col_recv, y_send, y_recv, fwd_send, fwd_recv) = (
            line_refs[2 * (line - 1) :]
        )
        sources = [sorted(range(line), key=lambda s, at=at: (abs(s - at), s)) for at in range(line)]
        core_cols = pl.ds(pl.multiple_of(core * half, half), half)
        core_rope = pl.ds(pl.multiple_of(core * rope_half, rope_half), rope_half)

        def source_of(n):
            code = sum(sources[at][n] << (4 * at) for at in range(line))
            return (code >> (4 * z)) & 15

        def to_line(at, target, src_lat, src_rope, source, send_sems):
            n = sources[target].index(source) - 1
            device = (pool, target * 2 + y, core)
            return [
                pltpu.make_async_remote_copy(
                    src_ref=src,
                    dst_ref=dst,
                    send_sem=send_sems.at[part],
                    recv_sem=col_recv.at[n, part],
                    device_id=device,
                    device_id_type=MESH,
                )
                for part, (src, dst) in enumerate(
                    [(src_lat, col_lat[n]), (src_rope, col_rope[n])]
                )
            ]

        def own_copies(at):
            copies = []
            for side, target in enumerate((at - 1, at + 1)):
                if 0 <= target < line:
                    copies += to_line(
                        at,
                        target,
                        pool_lat.at[:, :, core_cols],
                        pool_rope.at[:, core_rope, :],
                        at,
                        own_send.at[side],
                    )
            return copies

        def relay_copies(at, n):
            source = sources[at][n]
            target = at + 1 if source < at else at - 1
            if not 0 <= target < line:
                return []
            return to_line(
                at, target, col_lat[n - 1], col_rope[n - 1], source, relay_send.at[n - 1]
            )

        def arrive(at, n):
            for part, buf in enumerate((col_lat[n - 1], col_rope[n - 1])):
                pltpu.make_async_copy(buf, buf, col_recv.at[n - 1, part]).wait()
            for copy in relay_copies(at, n):
                copy.start()

        def each_place(body):
            for at in range(line):
                pl.when(z == at)(functools.partial(body, at))

        def greet(at):
            near = [t for t in (at - 1, at + 1) if 0 <= t < line]
            for t in near:
                pl.semaphore_signal(
                    barrier, inc=1, device_id=(pool, t * 2 + y, core), device_id_type=MESH
                )
            pl.semaphore_wait(barrier, len(near) + 2)

        barrier = pltpu.get_barrier_semaphore()
        pl.semaphore_signal(barrier, inc=1, device_id=partner, device_id_type=MESH)
        pl.semaphore_signal(barrier, inc=1, device_id=sibling, device_id_type=MESH)
        make_tables()
        each_place(greet)
        table_copy = pltpu.make_async_remote_copy(
            src_ref=table_ref,
            dst_ref=tables_in,
            send_sem=table_send.at[0],
            recv_sem=table_recv.at[0],
            device_id=partner,
            device_id_type=MESH,
        )
        table_copy.start()
        own_table = pltpu.make_async_copy(table_ref, table_smem, local_sem.at[len(pairs)])
        own_table.start()
        loads[0].wait()
        loads[1].wait()

        def send_own(at):
            for copy in own_copies(at):
                copy.start()

        each_place(send_own)
        own_table.wait()
        table_copy.wait_recv()
        partner_table = pltpu.make_async_copy(tables_in, tables_smem, local_sem.at[len(pairs)])
        partner_table.start()
        partner_table.wait()
        own_base = [toks + 2 * n * width for n in range(line)]
        y_base = [toks + (2 * n + 1) * width for n in range(line)]

        def y_copies(n):
            return [
                pltpu.make_async_remote_copy(
                    src_ref=src,
                    dst_ref=dst,
                    send_sem=y_send.at[n, part],
                    recv_sem=y_recv.at[n, part],
                    device_id=partner,
                    device_id_type=MESH,
                )
                for part, (src, dst) in enumerate(
                    [
                        (send_lat.at[n], kv.at[core, pl.ds(y_base[n], width), :]),
                        (send_rope.at[n], kr.at[core_rope, pl.ds(y_base[n], width)]),
                    ]
                )
            ]

        def pack_y(n):
            holder = source_of(n) * 2 + y
            for s in range(slots):
                b = tables_smem[holder, 0, s]
                rows = pl.ds(s * block, block)
                if n == 0:
                    send_lat[n, rows, :] = pool_lat[b, :, core_cols]
                    send_rope[n, :, rows] = pool_rope[b, core_rope, :]
                else:
                    send_lat[n, rows, :] = col_lat[n - 1][b]
                    send_rope[n, :, rows] = col_rope[n - 1][b]
            for copy in y_copies(n):
                copy.start()

        def sibling_copies(n, kind, start):
            lat_rows = kv.at[core, pl.ds(start, width), :]
            rope_rows = kr.at[core_rope, pl.ds(start, width)]
            return [
                pltpu.make_async_remote_copy(
                    src_ref=ref,
                    dst_ref=ref,
                    send_sem=fwd_send.at[n, kind, part],
                    recv_sem=fwd_recv.at[n, kind, part],
                    device_id=sibling,
                    device_id_type=MESH,
                )
                for part, ref in enumerate([lat_rows, rope_rows])
            ]

        def pack_own(n):
            holder = source_of(n) * 2 + y
            for s in range(slots):
                b = table_smem[holder, 0, s]
                rows = pl.ds(own_base[n] + s * block, block)
                kv[core, rows, :] = col_lat[n - 1][b]
                kr[core_rope, rows] = col_rope[n - 1][b]
            copies = sibling_copies(n, 0, own_base[n])
            for copy in copies:
                copy.start()
            return copies

        pack_y(0)
        own_row = me
        places = [(own_base[n], source_of(n) * 2 + y) for n in range(line)]
        places += [(y_base[n], source_of(n) * 2 + 1 - y) for n in range(line)]
    else:
        barrier = pltpu.get_barrier_semaphore()
        for k in order:
            pl.semaphore_signal(barrier, inc=1, device_id=peer(k), device_id_type=MESH)
        pl.semaphore_signal(barrier, inc=1, device_id=sibling, device_id_type=MESH)
        make_tables()
        pl.semaphore_wait(barrier, holders)

        tables = []
        for k in order:
            copy = pltpu.make_async_remote_copy(
                src_ref=table_ref.at[me ^ k],
                dst_ref=table_in.at[k],
                send_sem=table_send.at[k],
                recv_sem=table_recv.at[k],
                device_id=peer(k),
                device_id_type=MESH,
            )
            copy.start()
            tables.append(copy)
        table_in[0] = table_ref[me]
        for copy in tables:
            copy.wait_recv()
        to_smem = pltpu.make_async_copy(table_in, table_smem, local_sem.at[len(pairs)])
        to_smem.start()
        to_smem.wait()

        copies = {}
        loads[0].wait()
        loads[1].wait()
        for k in order:
            for s in range(slots):
                b = table_smem[k, 0, s]
                rows = pl.ds(s * block, block)
                send_lat[k, rows, :] = pool_lat[b, :, pl.ds(pl.multiple_of(core * half, half), half)]
                send_rope[k, :, rows] = pool_rope[
                    b, pl.ds(pl.multiple_of(core * rope_half, rope_half), rope_half), :
                ]
            lat_copy = pltpu.make_async_remote_copy(
                src_ref=send_lat.at[k],
                dst_ref=kv.at[core, pl.ds(base[k], width), :],
                send_sem=lat_send.at[k],
                recv_sem=lat_recv.at[k],
                device_id=peer(k),
                device_id_type=MESH,
            )
            rope_copy = pltpu.make_async_remote_copy(
                src_ref=send_rope.at[k],
                dst_ref=kr.at[
                    pl.ds(pl.multiple_of(core * rope_half, rope_half), rope_half), pl.ds(base[k], width)
                ],
                send_sem=rope_send.at[k],
                recv_sem=rope_recv.at[k],
                device_id=peer(k),
                device_id_type=MESH,
            )
            lat_copy.start()
            rope_copy.start()
            copies[k] = (lat_copy, rope_copy)
        own_row = 0
        places = [(base[k], me ^ k) for k in [0] + order]

    for at in range(2, 7):
        loads[at].wait()
    for c in range(2):
        kv[c, pl.ds(0, toks), :] = span_lat[:, c * half : (c + 1) * half]
    kr[pl.ds(0, rope), pl.ds(0, toks)] = span_rope[...]
    kr[pl.ds(rope, 128 - rope), :] = jnp.zeros((128 - rope, kr.shape[1]), jnp.bfloat16)
    for s in range(slots):
        b = table_smem[own_row, 0, s]
        for c in range(2):
            kv[c, pl.ds(toks + s * block, block), :] = pool_lat[b, :, c * half : (c + 1) * half]
        kr[pl.ds(0, rope), pl.ds(toks + s * block, block)] = pool_rope[b]
    top_row = lax.broadcasted_iota(jnp.int32, (16, width), 0) == 0
    for start, holder in places:
        row = bias_ref[pl.ds(holder, 1), :]
        kr[pl.ds(rope, 16), pl.ds(start, width)] = jnp.where(top_row, row, 0.0).astype(jnp.bfloat16)

    nope32[...] = nope[...].astype(jnp.float32)
    one_col = (lax.broadcasted_iota(jnp.int32, (toks, 128 - rope), 1) == 0).astype(jnp.bfloat16)
    for h in range(heads):
        q_h = nope32[pl.ds(h, toks, stride=heads), :].astype(jnp.bfloat16)
        up = jnp.dot(q_h, key_up[h], preferred_element_type=jnp.float32)
        q_all[pl.ds(h * toks, toks), 0:lat] = (up * scale).astype(jnp.bfloat16)
        rot = rope_q[:, h * rope : (h + 1) * rope].astype(jnp.float32) * scale
        q_all[pl.ds(h * toks, toks), lat:] = jnp.concatenate(
            [rot.astype(jnp.bfloat16), one_col], axis=1
        )

    tile = 16 * toks
    part = 2 * toks
    tiles = heads // 16

    def attend(start, size, first):
        keys = pl.ds(start, size)
        for c in range(2):
            kt[c * half : (c + 1) * half, keys] = kv[c, keys, :].T

        def one(t, carry):
            parts = [
                pl.ds(pl.multiple_of(t * tile + at * part, part), part) for at in range(tile // part)
            ]
            scores = [
                jnp.dot(q_all[rows, :], kt[:, keys], preferred_element_type=jnp.float32)
                for rows in parts
            ]
            if first:
                row = lax.broadcasted_iota(jnp.int32, (part, size), 0) % toks
                col = lax.broadcasted_iota(jnp.int32, (part, size), 1)
                seen = (col <= row) | (col >= toks)
                scores = [jnp.where(seen, s, MASKED) for s in scores]
            else:
                old = [peak[rows, :] for rows in parts]
                old_total = [total[rows, :] for rows in parts]
            tops, probs, sums, alphas = [], [], [], []
            for at, s in enumerate(scores):
                top = jnp.max(s, axis=1, keepdims=True)
                if not first:
                    top = jnp.maximum(top, old[at])
                    alphas.append(jnp.exp2(old[at] - top))
                p = jnp.exp2(s - top)
                tops.append(top)
                sums.append(jnp.sum(p, axis=1, keepdims=True))
                probs.append(p.astype(jnp.bfloat16))
            mixed = [
                [jnp.dot(p, kv[c, keys, :], preferred_element_type=jnp.float32) for c in range(2)]
                for p in probs
            ]
            for at, rows in enumerate(parts):
                peak[rows, :] = tops[at]
                total[rows, :] = sums[at] if first else old_total[at] * alphas[at] + sums[at]
                for c in range(2):
                    cols = pl.ds(c * half, half)
                    if first:
                        acc[rows, cols] = mixed[at][c]
                    else:
                        acc[rows, cols] = acc[rows, cols] * alphas[at] + mixed[at][c]
            return carry

        lax.fori_loop(0, tiles, one, 0)

    attend(0, toks + width, True)

    if line:
        forwards = []

        def take_y(n):
            for copy in y_copies(n):
                copy.wait_recv()
            copies = sibling_copies(n, 1, y_base[n])
            for copy in copies:
                copy.start()
            return copies

        for n in range(1, line):

            def arrivals(at, n=n):
                inner = 0 < at < line - 1
                ahead = [n] if not inner else [1, 2] if n == 1 else [n + 1]
                for m in ahead:
                    if m < line:
                        arrive(at, m)

            current = take_y(n - 1)
            each_place(arrivals)
            pack_y(n)
            current += pack_own(n)
            for copy in current:
                copy.wait_recv()
            forwards += current
            attend(y_base[n - 1], 2 * width, False)
        current = take_y(line - 1)
        for copy in current:
            copy.wait_recv()
        forwards += current
        attend(y_base[line - 1], width, False)
    else:
        forwards = []
        group = max(1, 768 // width)
        for at in range(0, len(order), group):
            members = order[at : at + group]
            current = []
            for k in members:
                copies[k][0].wait_recv()
                copies[k][1].wait_recv()
                lat_rows = kv.at[core, pl.ds(base[k], width), :]
                rope_rows = kr.at[
                    pl.ds(pl.multiple_of(core * rope_half, rope_half), rope_half), pl.ds(base[k], width)
                ]
                lat_fwd = pltpu.make_async_remote_copy(
                    src_ref=lat_rows,
                    dst_ref=lat_rows,
                    send_sem=fwd_lat_send.at[k],
                    recv_sem=fwd_lat_recv.at[k],
                    device_id=sibling,
                    device_id_type=MESH,
                )
                rope_fwd = pltpu.make_async_remote_copy(
                    src_ref=rope_rows,
                    dst_ref=rope_rows,
                    send_sem=fwd_rope_send.at[k],
                    recv_sem=fwd_rope_recv.at[k],
                    device_id=sibling,
                    device_id_type=MESH,
                )
                lat_fwd.start()
                rope_fwd.start()
                current += [lat_fwd, rope_fwd]
            for copy in current:
                copy.wait_recv()
            forwards += current
            attend(base[members[0]], len(members) * width, False)

    loads[7].wait()
    live = lax.broadcasted_iota(jnp.int32, (toks, value_up.shape[2]), 0) < count_ref[0]
    for h in range(heads):
        rows = pl.ds(h * toks, toks)
        mixed = (acc[rows, :] * (1.0 / total[rows, :])).astype(jnp.bfloat16)
        up = jnp.dot(mixed, value_up[h], preferred_element_type=jnp.float32)
        vdim = value_up.shape[2]
        out_ref[:, h * vdim : (h + 1) * vdim] = jnp.where(live, up, 0.0).astype(out_ref.dtype)

    if line:

        def drain(at):
            for copy in own_copies(at):
                copy.wait_send()
            for n in range(1, line):
                for copy in relay_copies(at, n):
                    copy.wait_send()

        each_place(drain)
        table_copy.wait_send()
        for n in range(line):
            for copy in y_copies(n):
                copy.wait_send()
        for copy in forwards:
            copy.wait_send()
    else:
        for copy in tables + forwards:
            copy.wait_send()
        for k in order:
            copies[k][0].wait_send()
            copies[k][1].wait_send()


def on_device(
    query_nope,
    query_rope,
    key_up,
    value_up,
    span_latent,
    span_rope,
    pool_latent,
    pool_rope,
    hit_holders,
    hit_blocks,
    prefix_len,
    span_len,
):
    holders = lax.axis_size("hold")
    toks, heads, nope_width = query_nope.shape
    lat = key_up.shape[2]
    rope = span_rope.shape[0]
    block = pool_latent.shape[1]
    list_len = hit_holders.shape[1]
    vdim = value_up.shape[2]
    slots = (list_len + holders - 1) // holders
    width = slots * block
    scale = float(nope_width + rope) ** (-0.5) * math.log2(math.e)

    keys = toks + holders * width
    rows = heads * toks
    vmem = pl.BlockSpec(memory_space=pltpu.VMEM)
    any_space = pl.BlockSpec(memory_space=pl.ANY)
    sems = pltpu.SemaphoreType.DMA((holders,))
    line = holders // 2 if holders <= 8 else 0
    line_scratch = []
    if line:
        stored = pool_latent.shape[0]
        line_scratch = [pltpu.VMEM((stored, block, lat // 2), jnp.bfloat16)] * (line - 1)
        line_scratch += [pltpu.VMEM((stored, rope // 2, block), jnp.bfloat16)] * (line - 1)
        line_scratch += [
            pltpu.VMEM((holders, 8, 128), jnp.int32),
            pltpu.SMEM((holders, 8, 128), jnp.int32),
            pltpu.SemaphoreType.DMA((2, 2)),
            pltpu.SemaphoreType.DMA((line, 2)),
            pltpu.SemaphoreType.DMA((line, 2)),
            pltpu.SemaphoreType.DMA((line, 2)),
            pltpu.SemaphoreType.DMA((line, 2)),
            pltpu.SemaphoreType.DMA((line, 2, 2)),
            pltpu.SemaphoreType.DMA((line, 2, 2)),
        ]
    sizes = (holders, slots, heads, toks, block, lat, rope, scale, line)
    return pl.pallas_call(
        functools.partial(kernel, sizes),
        out_shape=jax.ShapeDtypeStruct((toks, heads * vdim), jnp.bfloat16),
        in_specs=[pl.BlockSpec(memory_space=pltpu.SMEM)] * 3 + [any_space] * 10,
        out_specs=vmem,
        scratch_shapes=[
            pltpu.VMEM((holders, 8, 128), jnp.int32),
            pltpu.VMEM((holders, width), jnp.float32),
            pltpu.VMEM(hit_holders.shape, jnp.int32),
            pltpu.VMEM(hit_blocks.shape, jnp.int32),
            pltpu.VMEM(pool_latent.shape, jnp.bfloat16),
            pltpu.VMEM(pool_rope.shape, jnp.bfloat16),
            pltpu.VMEM(span_latent.shape, jnp.bfloat16),
            pltpu.VMEM(span_rope.shape, jnp.bfloat16),
            pltpu.VMEM(query_rope.shape, jnp.bfloat16),
            pltpu.VMEM((holders, 8, 128), jnp.int32),
            pltpu.SMEM((holders, 8, 128), jnp.int32),
            pltpu.VMEM((holders, width, lat // 2), jnp.bfloat16),
            pltpu.VMEM((holders, rope // 2, width), jnp.bfloat16),
            pltpu.VMEM((2, keys, lat // 2), jnp.bfloat16),
            pltpu.VMEM((lat + 128, keys), jnp.bfloat16),
            pltpu.VMEM((rows, nope_width), jnp.bfloat16),
            pltpu.VMEM((rows, nope_width), jnp.float32),
            pltpu.VMEM(key_up.shape, jnp.bfloat16),
            pltpu.VMEM(value_up.shape, jnp.bfloat16),
            pltpu.VMEM((rows, lat + 128), jnp.bfloat16),
            pltpu.VMEM((rows, lat), jnp.float32),
            pltpu.VMEM((rows, 1), jnp.float32),
            pltpu.VMEM((rows, 1), jnp.float32),
            pltpu.SemaphoreType.DMA((11,)),
        ]
        + [sems] * 10
        + line_scratch,
        compiler_params=pltpu.CompilerParams(
            collective_id=0, has_side_effects=True, vmem_limit_bytes=56 * 1024 * 1024
        ),
    )(
        hit_holders,
        prefix_len,
        span_len,
        hit_holders,
        hit_blocks,
        pool_latent,
        pool_rope,
        span_latent,
        span_rope,
        query_nope.reshape(rows, nope_width),
        query_rope,
        key_up,
        value_up,
    )


def solution(mesh):
    return jax.shard_map(
        on_device,
        mesh=mesh,
        in_specs=(
            P(("pool", "hold"), "head", None),
            P(("pool", "hold"), "head"),
            P("head", None, None),
            P("head", None, None),
            P(("pool", "hold"), None),
            P(None, ("pool", "hold")),
            P(("pool", "hold"), None, None),
            P(("pool", "hold"), None, None),
            P(("pool", "hold"), None),
            P(("pool", "hold"), None),
            P(("pool", "hold")),
            P(("pool", "hold")),
        ),
        out_specs=P(("pool", "hold"), "head"),
        check_vma=False,
    )
```
